256 devices in a mesh: rep: 4 (over z_lo), exp: 64 (over z_hi, y, x, core).
Axes of the slice: x: 4, y: 4, z: 8 (z_hi: 2, z_lo: 4; z = z_hi * 4 + z_lo), core: 2. Of those that a mesh axis runs over, the one named last changes fastest.
Arguments:
- tokens: bfloat16 [32768, 4096], P(('rep', 'exp')), may hold values from -6 to 6
- cotangent: bfloat16 [32768, 4096], P(('rep', 'exp')), may hold values from -6 to 6
- gates: bfloat16 [32768, 4, 2], P(('rep', 'exp')), may hold values from 0.099609375 to 1
- expert_ids: int32 [32768, 4, 2], P(('rep', 'exp')), may hold values from 0 to 127, as said below
- slots: int32 [32768, 4, 2], P(('rep', 'exp')), may hold values from 0 to 7, as said below
- w_gate: bfloat16 [128, 1024, 1024], P('exp', None, 'rep'), may hold values from -0.1875 to 0.1875
- w_up: bfloat16 [128, 1024, 1024], P('exp', None, 'rep'), may hold values from -0.1875 to 0.1875
- w_down: bfloat16 [128, 1024, 1024], P('exp', 'rep'), may hold values from -0.1875 to 0.1875
Outputs:
- token_grads: bfloat16 [32768, 4096], P(('rep', 'exp'))
- grad_gate: bfloat16 [128, 1024, 1024], P('exp', None, 'rep')
- grad_up: bfloat16 [128, 1024, 1024], P('exp', None, 'rep')
- grad_down: bfloat16 [128, 1024, 1024], P('exp', 'rep')
The draws below stay inside these ranges and needn't reach their ends.
Inputs may be any that keep to these rules, and one draw needn't show every extreme that they name: `expert_ids`: the two experts of a sub-token differ. Every device's block holds more than 7 assignments to one expert. slots is the number of earlier assignments to the same expert among the 128 tokens of the same device (in the order of token, sub-token, choice), or 7 if that number is 7 or more, meaning the assignment is dropped.
All inputs are finite; a program needn't handle non-finite values.
Results may differ from the reference program's by a relative error of at most 0.015.
Values may be sent and summed in bfloat16 or wider, within the bound.
No kernel may reach another device: no remote copies, remote signals or barrier semaphores. Data moves between devices by JAX's collectives and lax.ppermute only.
A program may use at most 128 MiB of HBM per device.

```python
import math
import jax
import jax.numpy as jnp
from jax import lax

HEADS = 4
SUB = 1024
FF = 1024
TOK_DEV = 128
D = 4096
EXPERTS = 128
TOKENS = 32768
CAP = 7
N_REP = 4
N_EXP = 64


def routing(key):
    devices = TOKENS // TOK_DEV
    slot_count_total = TOK_DEV * HEADS
    keys = jax.random.split(key, 4)
    first_a = jax.random.randint(keys[0], (devices, slot_count_total), 0, EXPERTS)
    first_b = jax.random.randint(keys[1], (devices, slot_count_total), 0, EXPERTS)
    offset_all = jax.random.randint(keys[2], (), 0, EXPERTS)
    first = (jnp.minimum(first_a, first_b) + offset_all) % EXPERTS
    first = first.at[:, :CAP + 1].set(jnp.broadcast_to(first[:, :1], (devices, CAP + 1)))
    offset = jax.random.randint(keys[3], (devices, slot_count_total), 1, EXPERTS)
    second = (first + offset) % EXPERTS
    flat = jnp.stack([first, second], -1).reshape(devices, slot_count_total * 2).astype(jnp.int32)
    onehot = (flat[:, :, None] == jnp.arange(EXPERTS, dtype=jnp.int32)[None, None, :]).astype(jnp.int32)
    rank = jnp.sum(jnp.cumsum(onehot, 1) * onehot, -1) - 1
    slot_all = jnp.minimum(rank, CAP).astype(jnp.int32)
    return (flat.reshape(TOKENS, HEADS, 2), slot_all.reshape(TOKENS, HEADS, 2))


def draw_expert_ids(key, part):
    chosen, placed = routing(key)
    return chosen


def draw_slots(key, part):
    chosen, placed = routing(key)
    return placed


def shard_levels(rng, dims, shards, least, top_value):
    def one(axis_at, blocks):
        heights = jax.random.uniform(jax.random.fold_in(jax.random.fold_in(rng, 6), axis_at), (blocks,), jnp.float32, least / len(shards), top_value / len(shards))
        return jnp.repeat(jnp.exp(heights), dims[axis_at] // blocks).reshape((-1,) + (1,) * (len(dims) - axis_at - 1))

    level = one(*shards[0])
    for cut in shards[1:]:
        level = level * one(*cut)
    return level


def scatter_about(rng, shape, deviation, most, pieces=(), held_as=jnp.bfloat16):
    gain = shard_levels(rng, shape, pieces, -0.22, 0.18) if pieces else 1.0
    entries = jax.random.normal(rng, shape, jnp.float32) * deviation * gain
    return jnp.minimum(jnp.maximum(entries, -most), most).astype(held_as)


def setup_inputs(seed: int = 0) -> dict:
    key_list = jax.random.split(jax.random.key(seed), 9)
    return {
        "tokens": scatter_about(key_list[0], (TOKENS, D), 1.0, 6.0, ((0, 256),)),
        "cotangent": scatter_about(key_list[1], (TOKENS, D), 1.0, 6.0, ((0, 256),)),
        "gates": jnp.clip(jnp.exp(math.log(1.0) - 2.306499 * jax.random.uniform(key_list[2], (TOKENS, HEADS, 2), jnp.float32) ** shard_levels(key_list[2], (TOKENS, HEADS, 2), ((0, 256),), -0.2, 0.2)), 0.099609375, 1.0).astype(jnp.bfloat16),
        "expert_ids": draw_expert_ids(jax.random.fold_in(key_list[8], 71), 0),
        "slots": draw_slots(jax.random.fold_in(key_list[8], 71), 0),
        "w_gate": scatter_about(key_list[5], (EXPERTS, SUB, FF), SUB ** -0.5, 0.1875, ((0, 64), (2, 4))),
        "w_up": scatter_about(key_list[6], (EXPERTS, SUB, FF), SUB ** -0.5, 0.1875, ((0, 64), (2, 4))),
        "w_down": scatter_about(key_list[7], (EXPERTS, FF, SUB), FF ** -0.5, 0.1875, ((0, 64), (1, 4))),
    }


def expert_pass(x_rows, dy_rows, wg, wu, wd):
    g = jnp.dot(x_rows, wg, preferred_element_type=jnp.float32)
    u = jnp.dot(x_rows, wu, preferred_element_type=jnp.float32)
    sig = jax.nn.sigmoid(g)
    act = g * sig
    hidden = (act * u).astype(jnp.bfloat16)
    dh = jnp.dot(dy_rows, wd.T, preferred_element_type=jnp.float32)
    up_weight_gradient = (dh * act).astype(jnp.bfloat16)
    gate_weight_gradient = (dh * u * sig * (1.0 + g * (1.0 - sig))).astype(jnp.bfloat16)
    grad_g = jnp.dot(x_rows.T, gate_weight_gradient, preferred_element_type=jnp.float32).astype(jnp.bfloat16)
    grad_u = jnp.dot(x_rows.T, up_weight_gradient, preferred_element_type=jnp.float32).astype(jnp.bfloat16)
    grad_d = jnp.dot(hidden.T, dy_rows, preferred_element_type=jnp.float32).astype(jnp.bfloat16)
    slot_count_total = x_rows.shape[0]
    hidden_width = FF // N_REP
    partition_pieces = jnp.einsum('jge,xge->gjx', gate_weight_gradient.reshape(slot_count_total, N_REP, hidden_width).astype(jnp.float32),
                       wg.reshape(SUB, N_REP, hidden_width).astype(jnp.float32))
    partition_pieces = partition_pieces + jnp.einsum('jge,xge->gjx', up_weight_gradient.reshape(slot_count_total, N_REP, hidden_width).astype(jnp.float32),
                               wu.reshape(SUB, N_REP, hidden_width).astype(jnp.float32))
    partition_pieces = lax.optimization_barrier(partition_pieces.astype(jnp.bfloat16)).astype(jnp.float32)
    dx_rows = jnp.sum(partition_pieces, 0).astype(jnp.bfloat16)
    return dx_rows, grad_g, grad_u, grad_d


def reference(tokens, cotangent, gates, expert_ids, slots, w_gate, w_up, w_down):
    devices = N_REP * N_EXP
    rows = TOK_DEV * HEADS
    ec = EXPERTS * CAP
    x = tokens.reshape(devices, rows, SUB)
    dy = cotangent.reshape(devices, rows, SUB)
    ids = expert_ids.reshape(devices, rows * 2).astype(jnp.int32)
    sl = slots.reshape(devices, rows * 2).astype(jnp.int32)
    gt = gates.reshape(devices, rows * 2).astype(jnp.float32)
    target = jnp.where(sl < CAP, ids * CAP + sl, ec).astype(jnp.int32)
    row_of = jnp.broadcast_to(jnp.repeat(jnp.arange(rows, dtype=jnp.int32), 2), (devices, rows * 2))
    dev = jnp.arange(devices, dtype=jnp.int32)[:, None]
    inverse_permutation = jnp.full((devices, ec + 1), rows, jnp.int32).at[dev, target].set(row_of)[:, :ec]
    gate_slot = jnp.zeros((devices, ec + 1), jnp.float32).at[dev, target].set(gt)[:, :ec]
    xpad = jnp.concatenate([x, jnp.zeros((devices, 1, SUB), jnp.bfloat16)], 1)
    dypad = jnp.concatenate([dy, jnp.zeros((devices, 1, SUB), jnp.bfloat16)], 1)
    pick = jax.vmap(lambda table, index: table[index])
    x_slot = pick(xpad, inverse_permutation)
    dy_slot = (gate_slot[:, :, None] * pick(dypad, inverse_permutation).astype(jnp.float32)).astype(jnp.bfloat16)
    x_slot = x_slot.reshape(devices, EXPERTS, CAP, SUB).transpose(1, 0, 2, 3).reshape(EXPERTS, devices * CAP, SUB)
    dy_slot = dy_slot.reshape(devices, EXPERTS, CAP, SUB).transpose(1, 0, 2, 3).reshape(EXPERTS, devices * CAP, SUB)
    dx_slot, grad_gate, grad_up, grad_down = lax.map(lambda item: expert_pass(*item),
                                                     (x_slot, dy_slot, w_gate, w_up, w_down))
    dx_slot = dx_slot.reshape(EXPERTS, devices, CAP, SUB).transpose(1, 0, 2, 3).reshape(devices, ec, SUB)
    dx_pad = jnp.concatenate([dx_slot, jnp.zeros((devices, 1, SUB), jnp.bfloat16)], 1)
    picked = pick(dx_pad, target).astype(jnp.float32)
    token_grads = jnp.sum(picked.reshape(devices, rows, 2, SUB), 2).reshape(TOKENS, D).astype(jnp.bfloat16)
    return token_grads, grad_gate, grad_up, grad_down
```

```python
import jax
import jax.numpy as jnp
from jax import lax
from jax.sharding import Mesh
from jax.sharding import PartitionSpec as P

HEADS = 4
CAP = 7
AXES = ("rep", "zh", "y", "x", "core")
EXP = ("zh", "y", "x", "core")
HOST = ("zh", "y", "x", "rep")
PAIR = ("rep", "core")


def to_host(q):
    return [
        (h * 2 + k, (2 * k + (h + q) % 2) * 2 + h // 2) for h in range(4) for k in range(2)
    ]


def from_host(q):
    return [(b, a) for a, b in to_host(q)]


SWAP = [(0, 1), (1, 0)]


def on_device(tokens, cotangent, gates, expert_ids, slots, w_gate, w_up, w_down):
    f32, bf16 = jnp.float32, jnp.bfloat16
    width = w_gate.shape[1]
    toks = tokens.shape[0]
    rows = toks * HEADS
    experts = 128
    ec = experts * CAP
    h = lax.axis_index("rep")

    pieces = []
    for q in range(2):
        p = (h + q) % 2
        piece = [lax.dynamic_index_in_dim(w, p, 0, keepdims=False) for w in (w_gate, w_up, w_down)]
        pieces.append([lax.ppermute(w, PAIR, to_host(q)) for w in piece])
    own = [
        jnp.concatenate([pieces[0][0], pieces[1][0]], 1),
        jnp.concatenate([pieces[0][1], pieces[1][1]], 1),
        jnp.concatenate([pieces[0][2], pieces[1][2]], 0),
    ]
    other = [lax.ppermute(w, "core", SWAP) for w in own]
    wg = jnp.concatenate([own[0], other[0]], 1)
    wu = jnp.concatenate([own[1], other[1]], 1)
    wd = jnp.concatenate([own[2], other[2]], 0)

    def heads_first(a):
        return jnp.transpose(a, (1, 0, 2)).reshape(rows, 2)

    ids = heads_first(expert_ids)
    slot = heads_first(slots)
    gate = heads_first(gates)
    target = jnp.where(slot < CAP, ids * CAP + slot, ec)
    place = lax.broadcasted_iota(jnp.int32, (ec, rows), 0)
    hit0 = target[:, 0][None, :] == place
    hit1 = target[:, 1][None, :] == place
    zero = jnp.zeros((), bf16)
    pick = (hit0 | hit1).astype(bf16)
    pick_gate = jnp.where(hit0, gate[:, 0][None, :], jnp.where(hit1, gate[:, 1][None, :], zero))

    def cut(a):
        return jnp.concatenate([a[:, i * width : (i + 1) * width] for i in range(HEADS)], 0)

    x_slot = jnp.dot(pick, cut(tokens), preferred_element_type=f32).astype(bf16)
    dy_slot = jnp.dot(pick_gate, cut(cotangent), preferred_element_type=f32).astype(bf16)

    def exchange(a):
        a = lax.all_to_all(a.reshape(experts, CAP, width), HOST, 0, 0, tiled=True)
        return a.reshape(ec, width)

    x = exchange(x_slot)
    dy = exchange(dy_slot)

    g = jnp.dot(x, wg, preferred_element_type=f32)
    u = jnp.dot(x, wu, preferred_element_type=f32)
    sig = jax.nn.sigmoid(g)
    act = g * sig
    hidden = (act * u).astype(bf16)
    dh = lax.dot_general(dy, wd, (((1,), (1,)), ((), ())), preferred_element_type=f32)
    d_up = (dh * act).astype(bf16)
    d_gate = (dh * u * sig * (1.0 + g * (1.0 - sig))).astype(bf16)
    over_hidden = (((1,), (1,)), ((), ()))
    dx = lax.dot_general(d_gate, wg, over_hidden, preferred_element_type=f32)
    dx = dx + lax.dot_general(d_up, wu, over_hidden, preferred_element_type=f32)
    returned = exchange(dx.astype(bf16))

    over_rows = (((0,), (0,)), ((), ()))

    def grads(a, b, axis):
        whole = lax.dot_general(a, b, over_rows, preferred_element_type=f32)
        mine, theirs = jnp.split(whole, 2, axis)
        mine = mine + lax.ppermute(theirs.astype(bf16), "core", SWAP).astype(f32)
        return jnp.split(mine.astype(bf16), 2, axis)

    back = []
    even = h % 2 == 0
    for a, b, axis in ((x, d_gate, 1), (x, d_up, 1), (hidden, dy, 0)):
        part = grads(a, b, axis)
        got = [lax.ppermute(part[q], PAIR, from_host(q)) for q in range(2)]
        back.append(
            jnp.stack([jnp.where(even, got[0], got[1]), jnp.where(even, got[1], got[0])], 0)
        )

    summed = lax.dot_general(pick, returned, over_rows, preferred_element_type=f32).astype(bf16)
    token_grads = jnp.concatenate([summed[i * toks : (i + 1) * toks] for i in range(HEADS)], 1)
    return (token_grads, back[0], back[1], back[2])


def solution(mesh):
    fine = Mesh(mesh.devices.reshape(4, 2, 4, 4, 2), AXES)
    by_token = ("rep",) + EXP
    return jax.shard_map(
        on_device,
        mesh=fine,
        in_specs=(
            P(by_token, None),
            P(by_token, None),
            P(by_token, None, None),
            P(by_token, None, None),
            P(by_token, None, None),
            P(EXP, None, "rep"),
            P(EXP, None, "rep"),
            P(EXP, "rep", None),
        ),
        out_specs=(
            P(by_token, None),
            P(EXP, None, "rep"),
            P(EXP, None, "rep"),
            P(EXP, "rep", None),
        ),
        check_vma=False,
    )
```

```python
import jax
import jax.numpy as jnp
from jax import lax
from jax.experimental import pallas as pl
from jax.experimental.pallas import tpu as pltpu
from jax.sharding import Mesh
from jax.sharding import PartitionSpec as P

HEADS = 4
CAP = 7
EXPERTS = 128
SUB = 1024
PART = 256
STEP = 448
ROWS = EXPERTS * CAP
AXES = ("rep", "zh", "y", "x", "core")
EXP = ("zh", "y", "x", "core")
HOST = ("zh", "y", "x", "rep")
PAIR = ("rep", "core")
SWAP = [(0, 1), (1, 0)]
F32, BF16 = jnp.float32, jnp.bfloat16


def to_host(q):
    return [
        (h * 2 + k, (2 * k + (h + q) % 2) * 2 + h // 2) for h in range(4) for k in range(2)
    ]


def from_host(q):
    return [(b, a) for a, b in to_host(q)]


def tall(down):
    return jnp.concatenate([down[:, i * PART : (i + 1) * PART] for i in range(SUB // PART)], 0)


def wide(stack):
    return jnp.concatenate([stack[i * PART : (i + 1) * PART] for i in range(SUB // PART)], 1)


def dot(a, b, over):
    return lax.dot_general(a, b, ((over[:1], over[1:]), ((), ())), preferred_element_type=F32)


def expert_kernel(x_ref, dy_ref, own_ref, other_ref, dx_ref, dg_ref, du_ref, hid_ref, sum_ref):
    j = pl.program_id(0)

    def part(w_ref):
        def step(i, _):
            at = pl.ds(pl.multiple_of(i * STEP, STEP), STEP)
            x = x_ref[at, :]
            g = dot(x, w_ref[0, :SUB, :], (1, 0))
            u = dot(x, w_ref[0, SUB : 2 * SUB, :], (1, 0))
            dh = jnp.zeros((STEP, PART), F32)
            for f in range(SUB // PART):
                low = 2 * SUB + f * PART
                dh += dot(
                    dy_ref[at, f * PART : (f + 1) * PART], w_ref[0, low : low + PART, :], (1, 1)
                )
            sig = jax.nn.sigmoid(g)
            act = g * sig
            hid_ref[at, :] = (act * u).astype(BF16)
            d_up = (dh * act).astype(BF16)
            d_gate = (dh * u * sig * (1.0 + g * (1.0 - sig))).astype(BF16)
            du_ref[at, :] = d_up
            dg_ref[at, :] = d_gate
            term = dot(d_gate, w_ref[0, :SUB, :], (1, 1)) + dot(
                d_up, w_ref[0, SUB : 2 * SUB, :], (1, 1)
            )

            @pl.when(j == 0)
            def _():
                sum_ref[at, :] = term

            @pl.when(j > 0)
            def _():
                sum_ref[at, :] += term

            return 0

        lax.fori_loop(0, ROWS // STEP, step, 0)

    @pl.when(j < 2)
    def _():
        part(own_ref)

    @pl.when(j >= 2)
    def _():
        part(other_ref)

    @pl.when(j == 3)
    def _():
        dx_ref[...] = sum_ref[...].astype(BF16)


def expert(x, dy, own, other):
    whole = pl.BlockSpec((ROWS, SUB), lambda j: (0, 0))
    columns = pl.BlockSpec((ROWS, PART), lambda j: (0, j))
    out = jax.ShapeDtypeStruct((ROWS, SUB), BF16)
    return pl.pallas_call(
        expert_kernel,
        grid=(4,),
        in_specs=[
            whole,
            whole,
            pl.BlockSpec((1, 3 * SUB, PART), lambda j: (jnp.minimum(j, 1), 0, 0)),
            pl.BlockSpec((1, 3 * SUB, PART), lambda j: (jnp.maximum(j - 2, 0), 0, 0)),
        ],
        out_specs=[whole, columns, columns, columns],
        out_shape=[out] * 4,
        scratch_shapes=[pltpu.VMEM((ROWS, SUB), F32)],
        compiler_params=pltpu.CompilerParams(
            dimension_semantics=("arbitrary",), vmem_limit_bytes=48 * 1024 * 1024
        ),
        cost_estimate=pl.CostEstimate(
            flops=10 * ROWS * SUB * SUB, bytes_accessed=18 * 2**20, transcendentals=ROWS * SUB
        ),
    )(x, dy, own, other)


def on_device(tokens, cotangent, gates, expert_ids, slots, w_gate, w_up, w_down):
    toks = tokens.shape[0]
    rows = toks * HEADS
    h = lax.axis_index("rep")

    packed = jnp.stack(
        [jnp.concatenate([w_gate[p], w_up[p], tall(w_down[p])], 0) for p in range(2)], 0
    )
    own = jnp.stack(
        [
            lax.ppermute(
                lax.dynamic_index_in_dim(packed, (h + q) % 2, 0, keepdims=False), PAIR, to_host(q)
            )
            for q in range(2)
        ],
        0,
    )
    other = lax.ppermute(own, "core", SWAP)

    def heads_first(a):
        return jnp.transpose(a, (1, 0, 2)).reshape(rows, 2)

    ids = heads_first(expert_ids)
    slot = heads_first(slots)
    gate = heads_first(gates)
    target = jnp.where(slot < CAP, ids * CAP + slot, ROWS)
    place = lax.broadcasted_iota(jnp.int32, (ROWS, rows), 0)
    hit0 = target[:, 0][None, :] == place
    hit1 = target[:, 1][None, :] == place
    zero = jnp.zeros((), BF16)
    pick = (hit0 | hit1).astype(BF16)
    pick_gate = jnp.where(hit0, gate[:, 0][None, :], jnp.where(hit1, gate[:, 1][None, :], zero))

    def cut(a):
        return jnp.concatenate([a[:, i * SUB : (i + 1) * SUB] for i in range(HEADS)], 0)

    x_slot = dot(pick, cut(tokens), (1, 0)).astype(BF16)
    dy_slot = dot(pick_gate, cut(cotangent), (1, 0)).astype(BF16)

    lanes = CAP * SUB // 128
    sent = jnp.concatenate(
        [x_slot.reshape(EXPERTS, lanes, 128), dy_slot.reshape(EXPERTS, lanes, 128)], 1
    )
    got = lax.all_to_all(sent, HOST, 0, 0, tiled=True)
    x = got[:, :lanes].reshape(ROWS, SUB)
    dy = got[:, lanes:].reshape(ROWS, SUB)

    dx, d_gate, d_up, hidden = expert(x, dy, own, other)
    returned = lax.all_to_all(dx.reshape(EXPERTS, lanes, 128), HOST, 0, 0, tiled=True)
    returned = returned.reshape(ROWS, SUB)

    whole = (dot(x, d_gate, (0, 0)), dot(x, d_up, (0, 0)), dot(hidden, dy, (0, 0)))

    def pack(q):
        low, high = q * PART, (q + 1) * PART
        return jnp.concatenate(
            [whole[0][:, low:high], whole[1][:, low:high], tall(whole[2][low:high])], 0
        )

    theirs = lax.ppermute(jnp.stack([pack(2), pack(3)], 0).astype(BF16), "core", SWAP)
    back = [
        lax.ppermute((pack(q) + theirs[q].astype(F32)).astype(BF16), PAIR, from_host(q))
        for q in range(2)
    ]
    even = h % 2 == 0
    both = [jnp.where(even, back[0], back[1]), jnp.where(even, back[1], back[0])]
    grad_gate = jnp.stack([a[:SUB] for a in both], 0)
    grad_up = jnp.stack([a[SUB : 2 * SUB] for a in both], 0)
    grad_down = jnp.stack([wide(a[2 * SUB :]) for a in both], 0)

    summed = dot(pick, returned, (0, 0)).astype(BF16)
    token_grads = jnp.concatenate([summed[i * toks : (i + 1) * toks] for i in range(HEADS)], 1)
    return (token_grads, grad_gate, grad_up, grad_down)


def solution(mesh):
    fine = Mesh(mesh.devices.reshape(4, 2, 4, 4, 2), AXES)
    by_token = ("rep",) + EXP
    return jax.shard_map(
        on_device,
        mesh=fine,
        in_specs=(
            P(by_token, None),
            P(by_token, None),
            P(by_token, None, None),
            P(by_token, None, None),
            P(by_token, None, None),
            P(EXP, None, "rep"),
            P(EXP, None, "rep"),
            P(EXP, "rep", None),
        ),
        out_specs=(
            P(by_token, None),
            P(EXP, None, "rep"),
            P(EXP, None, "rep"),
            P(EXP, "rep", None),
        ),
        check_vma=False,
    )
```

```python
import jax
import jax.numpy as jnp
from jax import lax
from jax.experimental import pallas as pl
from jax.experimental.pallas import tpu as pltpu
from jax.sharding import Mesh
from jax.sharding import PartitionSpec as P

HEADS = 4
CAP = 7
EXPERTS = 128
SUB = 1024
PART = 256
STEP = 448
ROWS = EXPERTS * CAP
AXES = ("rep", "zh", "y", "x", "core")
EXP = ("zh", "y", "x", "core")
PAIR = ("rep", "core")
RING = ("rep", "zh")
PLANES = 8
YX = 16
BLOCK = YX * CAP
SWAP = [(0, 1), (1, 0)]
MOVES = ((0, 112), (4, 64), (-4, 48), (3, 112), (-3, 112), (2, 112), (-2, 112), (1, 112), (-1, 112))
SIZES = tuple(n for _, n in MOVES)
F32, BF16 = jnp.float32, jnp.bfloat16


def to_host(q):
    return [
        (h * 2 + k, (2 * k + (h + q) % 2) * 2 + h // 2) for h in range(4) for k in range(2)
    ]


def from_host(q):
    return [(b, a) for a, b in to_host(q)]


def hop(a, d):
    if d == 0:
        return a
    if abs(d) == PLANES // 2:
        return hop(hop(a, d // 2), d // 2)

    def at(z):
        return (z % 4) * 2 + z // 4

    return lax.ppermute(a, RING, [(at(z), at((z + d) % PLANES)) for z in range(PLANES)])


def tall(down):
    return jnp.concatenate([down[:, i * PART : (i + 1) * PART] for i in range(SUB // PART)], 0)


def wide(stack):
    return jnp.concatenate([stack[i * PART : (i + 1) * PART] for i in range(SUB // PART)], 1)


def dot(a, b, over):
    return lax.dot_general(a, b, ((over[:1], over[1:]), ((), ())), preferred_element_type=F32)


def gather_rows(refs, out_ref):
    at = 0
    for ref in refs:
        out_ref[at : at + ref.shape[0], :] = ref[...]
        at += ref.shape[0]


def forward_kernel(*refs):
    blocks, (own_ref, other_ref, x_ref, act_ref, fac_ref, hid_ref) = refs[:-6], refs[-6:]
    j = pl.program_id(0)

    @pl.when(j == 0)
    def _():
        gather_rows(blocks, x_ref)

    def part(w_ref):
        def step(i, _):
            at = pl.ds(pl.multiple_of(i * STEP, STEP), STEP)
            x = x_ref[at, :]
            g = dot(x, w_ref[0, :SUB, :], (1, 0))
            u = dot(x, w_ref[0, SUB : 2 * SUB, :], (1, 0))
            sig = jax.nn.sigmoid(g)
            act = g * sig
            act_ref[at, :] = act
            fac_ref[at, :] = u * sig * (1.0 + g * (1.0 - sig))
            hid_ref[at, :] = (act * u).astype(BF16)
            return 0

        lax.fori_loop(0, ROWS // STEP, step, 0)

    @pl.when(j < 2)
    def _():
        part(own_ref)

    @pl.when(j >= 2)
    def _():
        part(other_ref)


def backward_kernel(*refs):
    count = len(SIZES)
    blocks, refs = refs[:count], refs[count:]
    (own_ref, other_ref, act_ref, fac_ref, dy_ref, dg_ref, du_ref), refs = refs[:7], refs[7:]
    dx_refs, sum_ref = refs[:count], refs[count]
    j = pl.program_id(0)

    @pl.when(j == 0)
    def _():
        gather_rows(blocks, dy_ref)

    def part(w_ref):
        def step(i, _):
            at = pl.ds(pl.multiple_of(i * STEP, STEP), STEP)
            dh = jnp.zeros((STEP, PART), F32)
            for f in range(SUB // PART):
                low = 2 * SUB + f * PART
                dh += dot(
                    dy_ref[at, f * PART : (f + 1) * PART], w_ref[0, low : low + PART, :], (1, 1)
                )
            d_up = (dh * act_ref[at, :]).astype(BF16)
            d_gate = (dh * fac_ref[at, :]).astype(BF16)
            du_ref[at, :] = d_up
            dg_ref[at, :] = d_gate
            term = dot(d_gate, w_ref[0, :SUB, :], (1, 1)) + dot(
                d_up, w_ref[0, SUB : 2 * SUB, :], (1, 1)
            )

            @pl.when(j == 0)
            def _():
                sum_ref[at, :] = term

            @pl.when(j > 0)
            def _():
                sum_ref[at, :] += term

            return 0

        lax.fori_loop(0, ROWS // STEP, step, 0)

    @pl.when(j < 2)
    def _():
        part(own_ref)

    @pl.when(j >= 2)
    def _():
        part(other_ref)

    @pl.when(j == 3)
    def _():
        at = 0
        for ref in dx_refs:
            ref[...] = sum_ref[at : at + ref.shape[0], :].astype(BF16)
            at += ref.shape[0]


def fixed(rows):
    return pl.BlockSpec((rows, SUB), lambda j: (0, 0))


COLUMNS = pl.BlockSpec((ROWS, PART), lambda j: (0, j))
WEIGHTS = [
    pl.BlockSpec((1, 3 * SUB, PART), lambda j: (jnp.minimum(j, 1), 0, 0)),
    pl.BlockSpec((1, 3 * SUB, PART), lambda j: (jnp.maximum(j - 2, 0), 0, 0)),
]


def params():
    return pltpu.CompilerParams(
        dimension_semantics=("arbitrary",), vmem_limit_bytes=48 * 1024 * 1024
    )


def forward(blocks, own, other):
    wide_out = jax.ShapeDtypeStruct((ROWS, SUB), F32)
    slim_out = jax.ShapeDtypeStruct((ROWS, SUB), BF16)
    return pl.pallas_call(
        forward_kernel,
        grid=(4,),
        in_specs=[fixed(n) for n in SIZES] + WEIGHTS,
        out_specs=[fixed(ROWS), COLUMNS, COLUMNS, COLUMNS],
        out_shape=[slim_out, wide_out, wide_out, slim_out],
        compiler_params=params(),
        cost_estimate=pl.CostEstimate(
            flops=4 * ROWS * SUB * SUB, bytes_accessed=18 * 2**20, transcendentals=ROWS * SUB
        ),
    )(*blocks, own, other)


def backward(blocks, own, other, act, fac):
    slim_out = jax.ShapeDtypeStruct((ROWS, SUB), BF16)
    out = pl.pallas_call(
        backward_kernel,
        grid=(4,),
        in_specs=[fixed(n) for n in SIZES] + WEIGHTS + [COLUMNS, COLUMNS],
        out_specs=[fixed(ROWS), COLUMNS, COLUMNS] + [fixed(n) for n in SIZES],
        out_shape=[slim_out] * 3 + [jax.ShapeDtypeStruct((n, SUB), BF16) for n in SIZES],
        scratch_shapes=[pltpu.VMEM((ROWS, SUB), F32)],
        compiler_params=params(),
        cost_estimate=pl.CostEstimate(
            flops=6 * ROWS * SUB * SUB, bytes_accessed=24 * 2**20, transcendentals=0
        ),
    )(*blocks, own, other, act, fac)
    return out[0], out[1], out[2], out[3:]


def on_device(tokens, cotangent, gates, expert_ids, slots, w_gate, w_up, w_down):
    toks = tokens.shape[0]
    rows = toks * HEADS
    h = lax.axis_index("rep")

    packed = jnp.stack(
        [jnp.concatenate([w_gate[p], w_up[p], tall(w_down[p])], 0) for p in range(2)], 0
    )
    own = jnp.stack(
        [
            lax.ppermute(
                lax.dynamic_index_in_dim(packed, (h + q) % 2, 0, keepdims=False), PAIR, to_host(q)
            )
            for q in range(2)
        ],
        0,
    )
    other = lax.ppermute(own, "core", SWAP)

    def heads_first(a):
        return jnp.transpose(a, (1, 0, 2)).reshape(rows, 2)

    ids = heads_first(expert_ids)
    slot = heads_first(slots)
    gate = heads_first(gates)
    first = (((ids >> 2) & 15) * PLANES + (ids >> 6) * 4 + (ids & 3)) * CAP
    target = jnp.where(slot < CAP, first + slot, ROWS)
    place = lax.broadcasted_iota(jnp.int32, (ROWS, rows), 0)
    hit0 = target[:, 0][None, :] == place
    hit1 = target[:, 1][None, :] == place
    zero = jnp.zeros((), BF16)
    pick = (hit0 | hit1).astype(BF16)
    pick_gate = jnp.where(hit0, gate[:, 0][None, :], jnp.where(hit1, gate[:, 1][None, :], zero))

    def cut(a):
        return jnp.concatenate([a[:, i * SUB : (i + 1) * SUB] for i in range(HEADS)], 0)

    def in_plane(a):
        a = a.reshape(YX, PLANES * CAP, SUB)
        return lax.all_to_all(a, ("y", "x"), 0, 0, tiled=True).reshape(ROWS, SUB)

    z = lax.axis_index("zh") * 4 + h
    there, rank = [], []
    for d, n in MOVES:
        start = 64 if d == -4 else 0
        there += [d] * n
        rank += range(start, start + n)
    plane = (z + jnp.array(there, jnp.int32)) % PLANES
    rank = jnp.array(rank, jnp.int32)
    source = (rank // CAP) * (PLANES * CAP) + plane * CAP + rank % CAP
    regroup = (source[:, None] == jnp.arange(ROWS, dtype=jnp.int32)[None, :]).astype(BF16)

    def cut_moves(a):
        out, low = [], 0
        for n in SIZES:
            out.append(a[low : low + n])
            low += n
        return out

    x_slot = dot(pick, cut(tokens), (1, 0)).astype(BF16)
    dy_slot = dot(pick_gate, cut(cotangent), (1, 0)).astype(BF16)
    x_blocks = dot(regroup, in_plane(x_slot), (1, 0)).astype(BF16)
    x_blocks, dy_slot, own = lax.optimization_barrier((x_blocks, dy_slot, own))
    other = lax.ppermute(own, "core", SWAP)
    x_blocks = [hop(a, d) for a, (d, _) in zip(cut_moves(x_blocks), MOVES)]
    dy_blocks = dot(regroup, in_plane(dy_slot), (1, 0)).astype(BF16)
    dy_blocks = [hop(a, d) for a, (d, _) in zip(cut_moves(dy_blocks), MOVES)]

    x, act, fac, hidden = forward(x_blocks, own, other)
    dy, d_gate, d_up, dx_blocks = backward(dy_blocks, own, other, act, fac)
    back = [
        hop(a, -d // 2) if abs(d) == 4 else hop(a, -d) if abs(d) == 3 else a
        for a, (d, _) in zip(dx_blocks, MOVES)
    ]
    back[1:5], x, dy, d_gate, d_up, hidden = lax.optimization_barrier(
        (back[1:5], x, dy, d_gate, d_up, hidden)
    )
    back = [
        hop(a, -d // 2) if abs(d) == 4 else hop(a, -d) if abs(d) < 3 else a
        for a, (d, _) in zip(back, MOVES)
    ]
    back = dot(regroup, jnp.concatenate(back, 0), (0, 0)).astype(BF16)
    returned = in_plane(back)

    whole = (dot(x, d_gate, (0, 0)), dot(x, d_up, (0, 0)), dot(hidden, dy, (0, 0)))

    def pack(q):
        low, high = q * PART, (q + 1) * PART
        return jnp.concatenate(
            [whole[0][:, low:high], whole[1][:, low:high], tall(whole[2][low:high])], 0
        )

    theirs = lax.ppermute(jnp.stack([pack(2), pack(3)], 0).astype(BF16), "core", SWAP)
    back = [
        lax.ppermute((pack(q) + theirs[q].astype(F32)).astype(BF16), PAIR, from_host(q))
        for q in range(2)
    ]
    even = h % 2 == 0
    both = [jnp.where(even, back[0], back[1]), jnp.where(even, back[1], back[0])]
    grad_gate = jnp.stack([a[:SUB] for a in both], 0)
    grad_up = jnp.stack([a[SUB : 2 * SUB] for a in both], 0)
    grad_down = jnp.stack([wide(a[2 * SUB :]) for a in both], 0)

    summed = dot(pick, returned, (0, 0)).astype(BF16)
    token_grads = jnp.concatenate([summed[i * toks : (i + 1) * toks] for i in range(HEADS)], 1)
    return (token_grads, grad_gate, grad_up, grad_down)


def solution(mesh):
    fine = Mesh(mesh.devices.reshape(4, 2, 4, 4, 2), AXES)
    by_token = ("rep",) + EXP
    return jax.shard_map(
        on_device,
        mesh=fine,
        in_specs=(
            P(by_token, None),
            P(by_token, None),
            P(by_token, None, None),
            P(by_token, None, None),
            P(by_token, None, None),
            P(EXP, None, "rep"),
            P(EXP, None, "rep"),
            P(EXP, "rep", None),
        ),
        out_specs=(
            P(by_token, None),
            P(EXP, None, "rep"),
            P(EXP, None, "rep"),
            P(EXP, "rep", None),
        ),
        check_vma=False,
    )
```

```python
import jax
import jax.numpy as jnp
from jax import lax
from jax.experimental import pallas as pl
from jax.experimental.pallas import tpu as pltpu
from jax.sharding import Mesh
from jax.sharding import PartitionSpec as P

HEADS = 4
CAP = 7
EXPERTS = 128
SUB = 1024
PART = 256
STEP = 448
ROWS = EXPERTS * CAP
AXES = ("rep", "zh", "y", "x", "core")
EXP = ("zh", "y", "x", "core")
PAIR = ("rep", "core")
PLANES = 8
YX = 16
SWAP = [(0, 1), (1, 0)]
F32, BF16 = jnp.float32, jnp.bfloat16


def to_host(q):
    return [
        (h * 2 + k, (2 * k + (h + q) % 2) * 2 + h // 2) for h in range(4) for k in range(2)
    ]


def from_host(q):
    return [(b, a) for a, b in to_host(q)]


def tall(down):
    return jnp.concatenate([down[:, i * PART : (i + 1) * PART] for i in range(SUB // PART)], 0)


def wide(stack):
    return jnp.concatenate([stack[i * PART : (i + 1) * PART] for i in range(SUB // PART)], 1)


def dot(a, b, over):
    return lax.dot_general(a, b, ((over[:1], over[1:]), ((), ())), preferred_element_type=F32)


def forward_kernel(x_ref, own_ref, other_ref, act_ref, fac_ref, hid_ref, gt_ref, ut_ref, dt_ref):
    j = pl.program_id(0)

    def part(w_ref):
        def step(i, _):
            at = pl.ds(pl.multiple_of(i * STEP, STEP), STEP)
            x = x_ref[at, :]
            g = dot(x, w_ref[0, :SUB, :], (1, 0))
            u = dot(x, w_ref[0, SUB : 2 * SUB, :], (1, 0))
            sig = jax.nn.sigmoid(g)
            act = g * sig
            act_ref[at, :] = act
            fac_ref[at, :] = u * sig * (1.0 + g * (1.0 - sig))
            hid_ref[at, :] = (act * u).astype(BF16)
            return 0

        lax.fori_loop(0, ROWS // STEP, step, 0)
        gt_ref[...] = w_ref[0, :SUB, :].T
        ut_ref[...] = w_ref[0, SUB : 2 * SUB, :].T
        for f in range(SUB // PART):
            low = 2 * SUB + f * PART
            dt_ref[f * PART : (f + 1) * PART, :] = w_ref[0, low : low + PART, :].T

    @pl.when(j < 2)
    def _():
        part(own_ref)

    @pl.when(j >= 2)
    def _():
        part(other_ref)


def backward_kernel(dy_ref, act_ref, fac_ref, gt_ref, ut_ref, dt_ref, dg_ref, du_ref, dx_ref):
    dh = dot(dy_ref[...], dt_ref[...], (1, 0))
    du_ref[...] = (dh * act_ref[...]).astype(BF16)
    dg_ref[...] = (dh * fac_ref[...]).astype(BF16)
    dx = dot(dg_ref[...], gt_ref[...], (1, 0)) + dot(du_ref[...], ut_ref[...], (1, 0))
    dx_ref[...] = dx.astype(BF16)


def params():
    return pltpu.CompilerParams(
        dimension_semantics=("arbitrary",), vmem_limit_bytes=48 * 1024 * 1024
    )


def forward(x, own, other):
    columns = pl.BlockSpec((ROWS, PART), lambda j: (0, j))
    float_out = jax.ShapeDtypeStruct((ROWS, SUB), F32)
    square = jax.ShapeDtypeStruct((SUB, SUB), BF16)
    return pl.pallas_call(
        forward_kernel,
        grid=(4,),
        in_specs=[
            pl.BlockSpec((ROWS, SUB), lambda j: (0, 0)),
            pl.BlockSpec((1, 3 * SUB, PART), lambda j: (jnp.minimum(j, 1), 0, 0)),
            pl.BlockSpec((1, 3 * SUB, PART), lambda j: (jnp.maximum(j - 2, 0), 0, 0)),
        ],
        out_specs=[columns] * 3
        + [pl.BlockSpec((PART, SUB), lambda j: (j, 0))] * 2
        + [pl.BlockSpec((SUB, PART), lambda j: (0, j))],
        out_shape=[float_out, float_out, jax.ShapeDtypeStruct((ROWS, SUB), BF16)] + [square] * 3,
        compiler_params=params(),
        cost_estimate=pl.CostEstimate(
            flops=4 * ROWS * SUB * SUB, bytes_accessed=24 * 2**20, transcendentals=ROWS * SUB
        ),
    )(x, own, other)


def backward(dy, act, fac, gate_t, up_t, down_t):
    some = pl.BlockSpec((STEP, SUB), lambda i: (i, 0))
    square = pl.BlockSpec((SUB, SUB), lambda i: (0, 0))
    return pl.pallas_call(
        backward_kernel,
        grid=(ROWS // STEP,),
        in_specs=[some] * 3 + [square] * 3,
        out_specs=[some] * 3,
        out_shape=[jax.ShapeDtypeStruct((ROWS, SUB), BF16)] * 3,
        compiler_params=params(),
        cost_estimate=pl.CostEstimate(
            flops=6 * ROWS * SUB * SUB, bytes_accessed=20 * 2**20, transcendentals=0
        ),
    )(dy, act, fac, gate_t, up_t, down_t)


def on_device(tokens, cotangent, gates, expert_ids, slots, w_gate, w_up, w_down):
    toks = tokens.shape[0]
    rows = toks * HEADS
    h = lax.axis_index("rep")

    packed = jnp.stack(
        [jnp.concatenate([w_gate[p], w_up[p], tall(w_down[p])], 0) for p in range(2)], 0
    )
    own = jnp.stack(
        [
            lax.ppermute(
                lax.dynamic_index_in_dim(packed, (h + q) % 2, 0, keepdims=False), PAIR, to_host(q)
            )
            for q in range(2)
        ],
        0,
    )
    other = lax.ppermute(own, "core", SWAP)

    def heads_first(a):
        return jnp.transpose(a, (1, 0, 2)).reshape(rows, 2)

    ids = heads_first(expert_ids)
    slot = heads_first(slots)
    gate = heads_first(gates)
    first = (((ids >> 2) & 15) * PLANES + (ids >> 6) * 4 + (ids & 3)) * CAP
    target = jnp.where(slot < CAP, first + slot, ROWS)
    place = lax.broadcasted_iota(jnp.int32, (ROWS, rows), 0)
    hit0 = target[:, 0][None, :] == place
    hit1 = target[:, 1][None, :] == place
    zero = jnp.zeros((), BF16)
    pick = (hit0 | hit1).astype(BF16)
    pick_gate = jnp.where(hit0, gate[:, 0][None, :], jnp.where(hit1, gate[:, 1][None, :], zero))

    def cut(a):
        return jnp.concatenate([a[:, i * SUB : (i + 1) * SUB] for i in range(HEADS)], 0)

    def in_plane(a):
        a = a.reshape(YX, PLANES * CAP, SUB)
        return lax.all_to_all(a, ("y", "x"), 0, 0, tiled=True).reshape(ROWS, SUB)

    def along_z(a):
        a = a.reshape(PLANES, YX * CAP, SUB)
        return lax.all_to_all(a, ("zh", "rep"), 0, 0, tiled=True).reshape(ROWS, SUB)

    row = jnp.arange(ROWS, dtype=jnp.int32)
    plane, rest = row // (YX * CAP), row % (YX * CAP)
    source = (rest // CAP) * (PLANES * CAP) + plane * CAP + rest % CAP
    regroup = (source[:, None] == row[None, :]).astype(BF16)

    x_slot = dot(pick, cut(tokens), (1, 0)).astype(BF16)
    dy_slot = dot(pick_gate, cut(cotangent), (1, 0)).astype(BF16)
    x_rows = dot(regroup, in_plane(x_slot), (1, 0)).astype(BF16)
    dy_rows = dot(regroup, in_plane(dy_slot), (1, 0)).astype(BF16)
    x_rows, dy_rows, own = lax.optimization_barrier((x_rows, dy_rows, own))
    other = lax.ppermute(own, "core", SWAP)
    x = along_z(x_rows)
    act, fac, hidden, gate_t, up_t, down_t = forward(x, own, other)
    dy = along_z(dy_rows)
    d_gate, d_up, dx = backward(dy, act, fac, gate_t, up_t, down_t)
    dx = along_z(dx)

    whole = (dot(x, d_gate, (0, 0)), dot(x, d_up, (0, 0)), dot(hidden, dy, (0, 0)))

    def pack(q):
        low, high = q * PART, (q + 1) * PART
        return jnp.concatenate(
            [whole[0][:, low:high], whole[1][:, low:high], tall(whole[2][low:high])], 0
        )

    theirs = lax.ppermute(jnp.stack([pack(2), pack(3)], 0).astype(BF16), "core", SWAP)
    dx, theirs = lax.optimization_barrier((dx, theirs))
    back = [
        lax.ppermute((pack(q) + theirs[q].astype(F32)).astype(BF16), PAIR, from_host(q))
        for q in range(2)
    ]
    returned = in_plane(dot(regroup, dx, (0, 0)).astype(BF16))
    even = h % 2 == 0
    both = [jnp.where(even, back[0], back[1]), jnp.where(even, back[1], back[0])]
    grad_gate = jnp.stack([a[:SUB] for a in both], 0)
    grad_up = jnp.stack([a[SUB : 2 * SUB] for a in both], 0)
    grad_down = jnp.stack([wide(a[2 * SUB :]) for a in both], 0)

    summed = dot(pick, returned, (0, 0)).astype(BF16)
    token_grads = jnp.concatenate([summed[i * toks : (i + 1) * toks] for i in range(HEADS)], 1)
    return (token_grads, grad_gate, grad_up, grad_down)


def solution(mesh):
    fine = Mesh(mesh.devices.reshape(4, 2, 4, 4, 2), AXES)
    by_token = ("rep",) + EXP
    return jax.shard_map(
        on_device,
        mesh=fine,
        in_specs=(
            P(by_token, None),
            P(by_token, None),
            P(by_token, None, None),
            P(by_token, None, None),
            P(by_token, None, None),
            P(EXP, None, "rep"),
            P(EXP, None, "rep"),
            P(EXP, "rep", None),
        ),
        out_specs=(
            P(by_token, None),
            P(EXP, None, "rep"),
            P(EXP, None, "rep"),
            P(EXP, "rep", None),
        ),
        check_vma=False,
    )
```

```python
import jax
import jax.numpy as jnp
from jax import lax
from jax.experimental import pallas as pl
from jax.experimental.pallas import tpu as pltpu
from jax.sharding import Mesh
from jax.sharding import PartitionSpec as P

HEADS = 4
CAP = 7
EXPERTS = 128
SUB = 1024
PART = 256
STEP = 448
ROWS = EXPERTS * CAP
AXES = ("rep", "zh", "y", "x", "core")
EXP = ("zh", "y", "x", "core")
PAIR = ("rep", "core")
PLANES = 8
YX = 16
SWAP = [(0, 1), (1, 0)]
F32, BF16 = jnp.float32, jnp.bfloat16


def to_host(q):
    return [
        (h * 2 + k, (2 * k + (h + q) % 2) * 2 + h // 2) for h in range(4) for k in range(2)
    ]


def from_host(q):
    return [(b, a) for a, b in to_host(q)]


def tall(down):
    return jnp.concatenate([down[:, i * PART : (i + 1) * PART] for i in range(SUB // PART)], 0)


def wide(stack):
    return jnp.concatenate([stack[i * PART : (i + 1) * PART] for i in range(SUB // PART)], 1)


def dot(a, b, over):
    return lax.dot_general(a, b, ((over[:1], over[1:]), ((), ())), preferred_element_type=F32)


def forward_kernel(
    x_ref, w0, w1, w2, w3, act_ref, fac_ref, hid_ref, gt_ref, ut_ref, dt_ref, w_ref
):
    j = pl.program_id(0)
    for i, ref in enumerate((w0, w1, w2, w3)):

        @pl.when(j == i)
        def _():
            w_ref[...] = ref[...]

    def step(i, _):
        at = pl.ds(pl.multiple_of(i * STEP, STEP), STEP)
        x = x_ref[at, :]
        g = dot(x, w_ref[:SUB, :], (1, 0))
        u = dot(x, w_ref[SUB : 2 * SUB, :], (1, 0))
        sig = jax.nn.sigmoid(g)
        act = g * sig
        act_ref[at, :] = act
        fac_ref[at, :] = u * sig * (1.0 + g * (1.0 - sig))
        hid_ref[at, :] = (act * u).astype(BF16)
        return 0

    lax.fori_loop(0, ROWS // STEP, step, 0)
    gt_ref[...] = w_ref[:SUB, :].T
    ut_ref[...] = w_ref[SUB : 2 * SUB, :].T
    for f in range(SUB // PART):
        low = 2 * SUB + f * PART
        dt_ref[f * PART : (f + 1) * PART, :] = w_ref[low : low + PART, :].T


def backward_kernel(dy_ref, act_ref, fac_ref, gt_ref, ut_ref, dt_ref, dg_ref, du_ref, dx_ref):
    dh = dot(dy_ref[...], dt_ref[...], (1, 0))
    du_ref[...] = (dh * act_ref[...]).astype(BF16)
    dg_ref[...] = (dh * fac_ref[...]).astype(BF16)
    dx = dot(dg_ref[...], gt_ref[...], (1, 0)) + dot(du_ref[...], ut_ref[...], (1, 0))
    dx_ref[...] = dx.astype(BF16)


def params():
    return pltpu.CompilerParams(
        dimension_semantics=("arbitrary",), vmem_limit_bytes=48 * 1024 * 1024
    )


def forward(x, pieces):
    columns = pl.BlockSpec((ROWS, PART), lambda j: (0, j))
    float_out = jax.ShapeDtypeStruct((ROWS, SUB), F32)
    square = jax.ShapeDtypeStruct((SUB, SUB), BF16)
    return pl.pallas_call(
        forward_kernel,
        grid=(4,),
        in_specs=[
            pl.BlockSpec((ROWS, SUB), lambda j: (0, 0)),
        ]
        + [pl.BlockSpec((3 * SUB, PART), lambda j: (0, 0))] * 4,
        out_specs=[columns] * 3
        + [pl.BlockSpec((PART, SUB), lambda j: (j, 0))] * 2
        + [pl.BlockSpec((SUB, PART), lambda j: (0, j))],
        out_shape=[float_out, float_out, jax.ShapeDtypeStruct((ROWS, SUB), BF16)] + [square] * 3,
        scratch_shapes=[pltpu.VMEM((3 * SUB, PART), BF16)],
        compiler_params=params(),
        cost_estimate=pl.CostEstimate(
            flops=4 * ROWS * SUB * SUB, bytes_accessed=24 * 2**20, transcendentals=ROWS * SUB
        ),
    )(x, *pieces)


def backward(dy, act, fac, gate_t, up_t, down_t):
    some = pl.BlockSpec((STEP, SUB), lambda i: (i, 0))
    square = pl.BlockSpec((SUB, SUB), lambda i: (0, 0))
    return pl.pallas_call(
        backward_kernel,
        grid=(ROWS // STEP,),
        in_specs=[some] * 3 + [square] * 3,
        out_specs=[some] * 3,
        out_shape=[jax.ShapeDtypeStruct((ROWS, SUB), BF16)] * 3,
        compiler_params=params(),
        cost_estimate=pl.CostEstimate(
            flops=6 * ROWS * SUB * SUB, bytes_accessed=20 * 2**20, transcendentals=0
        ),
    )(dy, act, fac, gate_t, up_t, down_t)


def on_device(tokens, cotangent, gates, expert_ids, slots, w_gate, w_up, w_down):
    toks = tokens.shape[0]
    rows = toks * HEADS
    h = lax.axis_index("rep")

    own = []
    for q in range(2):
        one = [
            lax.dynamic_index_in_dim(w, (h + q) % 2, 0, keepdims=False)
            for w in (w_gate, w_up, w_down)
        ]
        piece = jnp.concatenate([one[0], one[1], tall(one[2])], 0)
        if own:
            piece, own[0] = lax.optimization_barrier((piece, own[0]))
        own.append(lax.ppermute(piece, PAIR, to_host(q)))

    def heads_first(a):
        return jnp.transpose(a, (1, 0, 2)).reshape(rows, 2)

    ids = heads_first(expert_ids)
    slot = heads_first(slots)
    gate = heads_first(gates)
    first = (((ids >> 2) & 15) * PLANES + (ids >> 6) * 4 + (ids & 3)) * CAP
    target = jnp.where(slot < CAP, first + slot, ROWS)
    place = lax.broadcasted_iota(jnp.int32, (ROWS, rows), 0)
    hit0 = target[:, 0][None, :] == place
    hit1 = target[:, 1][None, :] == place
    zero = jnp.zeros((), BF16)
    pick = (hit0 | hit1).astype(BF16)
    pick_gate = jnp.where(hit0, gate[:, 0][None, :], jnp.where(hit1, gate[:, 1][None, :], zero))

    def cut(a):
        return jnp.concatenate([a[:, i * SUB : (i + 1) * SUB] for i in range(HEADS)], 0)

    def in_plane(a):
        a = a.reshape(YX, PLANES * CAP, SUB)
        return lax.all_to_all(a, ("y", "x"), 0, 0, tiled=True).reshape(ROWS, SUB)

    def along_z(a):
        a = a.reshape(PLANES, YX * CAP, SUB)
        return lax.all_to_all(a, ("zh", "rep"), 0, 0, tiled=True).reshape(ROWS, SUB)

    row = jnp.arange(ROWS, dtype=jnp.int32)
    plane, rest = row // (YX * CAP), row % (YX * CAP)
    source = (rest // CAP) * (PLANES * CAP) + plane * CAP + rest % CAP
    regroup = (source[:, None] == row[None, :]).astype(BF16)

    x_slot = dot(pick, cut(tokens), (1, 0)).astype(BF16)
    dy_slot = dot(pick_gate, cut(cotangent), (1, 0)).astype(BF16)
    x_rows = dot(regroup, in_plane(x_slot), (1, 0)).astype(BF16)
    dy_rows = in_plane(dy_slot)
    x_rows, dy_rows, own = lax.optimization_barrier((x_rows, dy_rows, own))
    other = [lax.ppermute(w, "core", SWAP) for w in own]
    x = along_z(x_rows)
    act, fac, hidden, gate_t, up_t, down_t = forward(x, own + other)
    dy = along_z(dot(regroup, dy_rows, (1, 0)).astype(BF16))
    d_gate, d_up, dx = backward(dy, act, fac, gate_t, up_t, down_t)
    dx = along_z(dx)

    whole = (dot(x, d_gate, (0, 0)), dot(x, d_up, (0, 0)), dot(hidden, dy, (0, 0)))

    def pack(q):
        low, high = q * PART, (q + 1) * PART
        return jnp.concatenate(
            [whole[0][:, low:high], whole[1][:, low:high], tall(whole[2][low:high])], 0
        )

    theirs = lax.ppermute(jnp.stack([pack(2), pack(3)], 0).astype(BF16), "core", SWAP)
    sums = [(pack(q) + theirs[q].astype(F32)).astype(BF16) for q in range(2)]
    dx, sums = lax.optimization_barrier((dx, sums))
    first = lax.ppermute(sums[0], PAIR, from_host(0))
    first, second = lax.optimization_barrier((first, sums[1]))
    back = [first, lax.ppermute(second, PAIR, from_host(1))]
    returned = in_plane(dot(regroup, dx, (0, 0)).astype(BF16))
    even = h % 2 == 0
    both = [jnp.where(even, back[0], back[1]), jnp.where(even, back[1], back[0])]
    grad_gate = jnp.stack([a[:SUB] for a in both], 0)
    grad_up = jnp.stack([a[SUB : 2 * SUB] for a in both], 0)
    grad_down = jnp.stack([wide(a[2 * SUB :]) for a in both], 0)

    summed = dot(pick, returned, (0, 0)).astype(BF16)
    token_grads = jnp.concatenate([summed[i * toks : (i + 1) * toks] for i in range(HEADS)], 1)
    return (token_grads, grad_gate, grad_up, grad_down)


def solution(mesh):
    fine = Mesh(mesh.devices.reshape(4, 2, 4, 4, 2), AXES)
    by_token = ("rep",) + EXP
    return jax.shard_map(
        on_device,
        mesh=fine,
        in_specs=(
            P(by_token, None),
            P(by_token, None),
            P(by_token, None, None),
            P(by_token, None, None),
            P(by_token, None, None),
            P(EXP, None, "rep"),
            P(EXP, None, "rep"),
            P(EXP, "rep", None),
        ),
        out_specs=(
            P(by_token, None),
            P(EXP, None, "rep"),
            P(EXP, None, "rep"),
            P(EXP, "rep", None),
        ),
        check_vma=False,
    )
```

```python
import jax
import jax.numpy as jnp
from jax import lax
from jax.experimental import pallas as pl
from jax.experimental.pallas import tpu as pltpu
from jax.sharding import Mesh
from jax.sharding import PartitionSpec as P

HEADS = 4
CAP = 7
EXPERTS = 128
SUB = 1024
PART = 256
STEP = 448
ROWS = EXPERTS * CAP
AXES = ("rep", "zh", "y", "x", "core")
EXP = ("zh", "y", "x", "core")
PAIR = ("rep", "core")
PLANES = 8
YX = 16
SWAP = [(0, 1), (1, 0)]
F32, BF16 = jnp.float32, jnp.bfloat16


def to_host(q):
    return [
        (h * 2 + k, (2 * k + (h + q) % 2) * 2 + h // 2) for h in range(4) for k in range(2)
    ]


def from_host(q):
    return [(b, a) for a, b in to_host(q)]


def tall(down):
    return jnp.concatenate([down[:, i * PART : (i + 1) * PART] for i in range(SUB // PART)], 0)


def wide(stack):
    return jnp.concatenate([stack[i * PART : (i + 1) * PART] for i in range(SUB // PART)], 1)


def dot(a, b, over):
    return lax.dot_general(a, b, ((over[:1], over[1:]), ((), ())), preferred_element_type=F32)


def forward_kernel(
    x_ref, own_ref, other_ref, act_ref, fac_ref, hid_ref, gt_ref, ut_ref, dt_ref, w_ref
):
    j = pl.program_id(0)
    for i in range(4):

        @pl.when(j == i)
        def _():
            w_ref[...] = (own_ref, other_ref)[i // 2][i % 2]

    def step(i, _):
        at = pl.ds(pl.multiple_of(i * STEP, STEP), STEP)
        x = x_ref[at, :]
        g = dot(x, w_ref[:SUB, :], (1, 0))
        u = dot(x, w_ref[SUB : 2 * SUB, :], (1, 0))
        sig = jax.nn.sigmoid(g)
        act = g * sig
        act_ref[at, :] = act
        fac_ref[at, :] = u * sig * (1.0 + g * (1.0 - sig))
        hid_ref[at, :] = (act * u).astype(BF16)
        return 0

    lax.fori_loop(0, ROWS // STEP, step, 0)
    gt_ref[...] = w_ref[:SUB, :].T
    ut_ref[...] = w_ref[SUB : 2 * SUB, :].T
    for f in range(SUB // PART):
        low = 2 * SUB + f * PART
        dt_ref[f * PART : (f + 1) * PART, :] = w_ref[low : low + PART, :].T


def backward_kernel(dy_ref, act_ref, fac_ref, gt_ref, ut_ref, dt_ref, dg_ref, du_ref, dx_ref):
    dh = dot(dy_ref[...], dt_ref[...], (1, 0))
    du_ref[...] = (dh * act_ref[...]).astype(BF16)
    dg_ref[...] = (dh * fac_ref[...]).astype(BF16)
    dx = dot(dg_ref[...], gt_ref[...], (1, 0)) + dot(du_ref[...], ut_ref[...], (1, 0))
    dx_ref[...] = dx.astype(BF16)


def gradient_kernel(x_ref, dy_ref, dg_ref, du_ref, hid_ref, own_ref, theirs_ref, xt_ref):
    j = pl.program_id(0)

    @pl.when(j == 0)
    def _():
        xt_ref[...] = x_ref[...].T

    def part(out_ref):
        out_ref[0, :SUB, :] = dot(xt_ref[...], dg_ref[...], (1, 0)).astype(BF16)
        out_ref[0, SUB : 2 * SUB, :] = dot(xt_ref[...], du_ref[...], (1, 0)).astype(BF16)
        down = dot(hid_ref[...].T, dy_ref[...], (1, 0)).astype(BF16)
        for f in range(SUB // PART):
            low = 2 * SUB + f * PART
            out_ref[0, low : low + PART, :] = down[:, f * PART : (f + 1) * PART]

    @pl.when(j < 2)
    def _():
        part(own_ref)

    @pl.when(j >= 2)
    def _():
        part(theirs_ref)


def gradients(x, dy, d_gate, d_up, hidden):
    whole = pl.BlockSpec((ROWS, SUB), lambda j: (0, 0))
    columns = pl.BlockSpec((ROWS, PART), lambda j: (0, j))
    return pl.pallas_call(
        gradient_kernel,
        grid=(4,),
        in_specs=[whole, whole, columns, columns, columns],
        out_specs=[
            pl.BlockSpec((1, 3 * SUB, PART), lambda j: (jnp.minimum(j, 1), 0, 0)),
            pl.BlockSpec((1, 3 * SUB, PART), lambda j: (jnp.maximum(j - 2, 0), 0, 0)),
        ],
        out_shape=[jax.ShapeDtypeStruct((2, 3 * SUB, PART), BF16)] * 2,
        scratch_shapes=[pltpu.VMEM((SUB, ROWS), BF16)],
        compiler_params=params(),
        cost_estimate=pl.CostEstimate(flops=2**20, bytes_accessed=2**16, transcendentals=0),
    )(x, dy, d_gate, d_up, hidden)


def params():
    return pltpu.CompilerParams(
        dimension_semantics=("arbitrary",), vmem_limit_bytes=48 * 1024 * 1024
    )


def forward(x, own, other):
    columns = pl.BlockSpec((ROWS, PART), lambda j: (0, j))
    float_out = jax.ShapeDtypeStruct((ROWS, SUB), F32)
    square = jax.ShapeDtypeStruct((SUB, SUB), BF16)
    return pl.pallas_call(
        forward_kernel,
        grid=(4,),
        in_specs=[
            pl.BlockSpec((ROWS, SUB), lambda j: (0, 0)),
        ]
        + [pl.BlockSpec((2, 3 * SUB, PART), lambda j: (0, 0, 0))] * 2,
        out_specs=[columns] * 3
        + [pl.BlockSpec((PART, SUB), lambda j: (j, 0))] * 2
        + [pl.BlockSpec((SUB, PART), lambda j: (0, j))],
        out_shape=[float_out, float_out, jax.ShapeDtypeStruct((ROWS, SUB), BF16)] + [square] * 3,
        scratch_shapes=[pltpu.VMEM((3 * SUB, PART), BF16)],
        compiler_params=params(),
        cost_estimate=pl.CostEstimate(
            flops=4 * ROWS * SUB * SUB, bytes_accessed=24 * 2**20, transcendentals=ROWS * SUB
        ),
    )(x, own, other)


def backward(dy, act, fac, gate_t, up_t, down_t):
    some = pl.BlockSpec((STEP, SUB), lambda i: (i, 0))
    square = pl.BlockSpec((SUB, SUB), lambda i: (0, 0))
    return pl.pallas_call(
        backward_kernel,
        grid=(ROWS // STEP,),
        in_specs=[some] * 3 + [square] * 3,
        out_specs=[some] * 3,
        out_shape=[jax.ShapeDtypeStruct((ROWS, SUB), BF16)] * 3,
        compiler_params=params(),
        cost_estimate=pl.CostEstimate(
            flops=6 * ROWS * SUB * SUB, bytes_accessed=20 * 2**20, transcendentals=0
        ),
    )(dy, act, fac, gate_t, up_t, down_t)


def on_device(tokens, cotangent, gates, expert_ids, slots, w_gate, w_up, w_down):
    toks = tokens.shape[0]
    rows = toks * HEADS
    h = lax.axis_index("rep")

    stages = []
    for w in (w_gate, w_up, w_down):
        pair = [lax.dynamic_index_in_dim(w, (h + q) % 2, 0, keepdims=False) for q in range(2)]
        if stages:
            pair, stages[-1] = lax.optimization_barrier((pair, stages[-1]))
        stages.append([lax.ppermute(pair[q], PAIR, to_host(q)) for q in range(2)])

    def heads_first(a):
        return jnp.transpose(a, (1, 0, 2)).reshape(rows, 2)

    ids = heads_first(expert_ids)
    slot = heads_first(slots)
    gate = heads_first(gates)
    first = (((ids >> 2) & 15) * PLANES + (ids >> 6) * 4 + (ids & 3)) * CAP
    target = jnp.where(slot < CAP, first + slot, ROWS)
    place = lax.broadcasted_iota(jnp.int32, (ROWS, rows), 0)
    hit0 = target[:, 0][None, :] == place
    hit1 = target[:, 1][None, :] == place
    zero = jnp.zeros((), BF16)
    pick = (hit0 | hit1).astype(BF16)
    pick_gate = jnp.where(hit0, gate[:, 0][None, :], jnp.where(hit1, gate[:, 1][None, :], zero))

    def cut(a):
        return jnp.concatenate([a[:, i * SUB : (i + 1) * SUB] for i in range(HEADS)], 0)

    def in_plane(a):
        a = a.reshape(YX, PLANES * CAP, SUB)
        return lax.all_to_all(a, ("y", "x"), 0, 0, tiled=True).reshape(ROWS, SUB)

    def along_z(a):
        a = a.reshape(PLANES, YX * CAP, SUB)
        return lax.all_to_all(a, ("zh", "rep"), 0, 0, tiled=True).reshape(ROWS, SUB)

    row = jnp.arange(ROWS, dtype=jnp.int32)
    plane, rest = row // (YX * CAP), row % (YX * CAP)
    source = (rest // CAP) * (PLANES * CAP) + plane * CAP + rest % CAP
    regroup = (source[:, None] == row[None, :]).astype(BF16)

    x_slot = dot(pick, cut(tokens), (1, 0)).astype(BF16)
    dy_slot = dot(pick_gate, cut(cotangent), (1, 0)).astype(BF16)
    x_rows = dot(regroup, in_plane(x_slot), (1, 0)).astype(BF16)
    dy_rows = in_plane(dy_slot)
    x_rows, dy_rows, stages = lax.optimization_barrier((x_rows, dy_rows, stages))
    own = jnp.stack(
        [
            jnp.concatenate([stages[0][q], stages[1][q], tall(stages[2][q])], 0)
            for q in range(2)
        ],
        0,
    )
    other = lax.ppermute(own, "core", SWAP)
    x = along_z(x_rows)
    act, fac, hidden, gate_t, up_t, down_t = forward(x, own, other)
    dy = along_z(dot(regroup, dy_rows, (1, 0)).astype(BF16))
    d_gate, d_up, dx = backward(dy, act, fac, gate_t, up_t, down_t)
    dx = along_z(dx)

    mine, theirs = gradients(x, dy, d_gate, d_up, hidden)
    theirs = lax.ppermute(theirs, "core", SWAP)
    sums = [(mine[q].astype(F32) + theirs[q].astype(F32)).astype(BF16) for q in range(2)]
    dx, sums = lax.optimization_barrier((dx, sums))
    back = [lax.ppermute(sums[q], PAIR, from_host(q)) for q in range(2)]
    returned = in_plane(dot(regroup, dx, (0, 0)).astype(BF16))
    summed = dot(pick, returned, (0, 0)).astype(BF16)
    token_grads = jnp.concatenate([summed[i * toks : (i + 1) * toks] for i in range(HEADS)], 1)

    token_grads, back = lax.optimization_barrier((token_grads, back))
    even = h % 2 == 0
    both = [jnp.where(even, back[0], back[1]), jnp.where(even, back[1], back[0])]
    grad_gate = jnp.stack([a[:SUB] for a in both], 0)
    grad_up = jnp.stack([a[SUB : 2 * SUB] for a in both], 0)
    grad_down = jnp.stack([wide(a[2 * SUB :]) for a in both], 0)
    return (token_grads, grad_gate, grad_up, grad_down)


def solution(mesh):
    fine = Mesh(mesh.devices.reshape(4, 2, 4, 4, 2), AXES)
    by_token = ("rep",) + EXP
    return jax.shard_map(
        on_device,
        mesh=fine,
        in_specs=(
            P(by_token, None),
            P(by_token, None),
            P(by_token, None, None),
            P(by_token, None, None),
            P(by_token, None, None),
            P(EXP, None, "rep"),
            P(EXP, None, "rep"),
            P(EXP, "rep", None),
        ),
        out_specs=(
            P(by_token, None),
            P(EXP, None, "rep"),
            P(EXP, None, "rep"),
            P(EXP, "rep", None),
        ),
        check_vma=False,
    )
```

```python
import jax
import jax.numpy as jnp
from jax import lax
from jax.experimental import pallas as pl
from jax.experimental.pallas import tpu as pltpu
from jax.sharding import Mesh
from jax.sharding import PartitionSpec as P

HEADS = 4
CAP = 7
EXPERTS = 128
SUB = 1024
PART = 256
STEP = 448
ROWS = EXPERTS * CAP
AXES = ("rep", "zh", "y", "x", "core")
EXP = ("zh", "y", "x", "core")
PAIR = ("rep", "core")
PLANES = 8
YX = 16
SWAP = [(0, 1), (1, 0)]
F32, BF16 = jnp.float32, jnp.bfloat16


def to_host(q):
    return [
        (h * 2 + k, (2 * k + (h + q) % 2) * 2 + h // 2) for h in range(4) for k in range(2)
    ]


def from_host(q):
    return [(b, a) for a, b in to_host(q)]


def dot(a, b, over):
    return lax.dot_general(a, b, ((over[:1], over[1:]), ((), ())), preferred_element_type=F32)


def forward_kernel(
    x_ref, own_ref, other_ref, _, act_ref, fac_ref, hid_ref, gt_ref, ut_ref, dt_ref, xt_ref, w_ref
):
    j = pl.program_id(0)
    for i in range(4):

        @pl.when(j == i)
        def _():
            w_ref[...] = (own_ref, other_ref)[i // 2][i % 2]

    @pl.when(j == 0)
    def _():
        xt_ref[...] = x_ref[...].T

    def step(i, _):
        at = pl.ds(pl.multiple_of(i * STEP, STEP), STEP)
        x = x_ref[at, :]
        g = dot(x, w_ref[:SUB, :], (1, 0))
        u = dot(x, w_ref[SUB : 2 * SUB, :], (1, 0))
        sig = jax.nn.sigmoid(g)
        act = g * sig
        act_ref[at, :] = act
        fac_ref[at, :] = u * sig * (1.0 + g * (1.0 - sig))
        hid_ref[at, :] = (act * u).astype(BF16)
        return 0

    lax.fori_loop(0, ROWS // STEP, step, 0)
    gt_ref[...] = w_ref[:SUB, :].T
    ut_ref[...] = w_ref[SUB : 2 * SUB, :].T
    for f in range(SUB // PART):
        low = 2 * SUB + f * PART
        dt_ref[f * PART : (f + 1) * PART, :] = w_ref[low : low + PART, :].T


def backward_kernel(dy_ref, act_ref, fac_ref, gt_ref, ut_ref, dt_ref, dg_ref, du_ref, dx_ref):
    dh = dot(dy_ref[...], dt_ref[...], (1, 0))
    du_ref[...] = (dh * act_ref[...]).astype(BF16)
    dg_ref[...] = (dh * fac_ref[...]).astype(BF16)
    dx = dot(dg_ref[...], gt_ref[...], (1, 0)) + dot(du_ref[...], ut_ref[...], (1, 0))
    dx_ref[...] = dx.astype(BF16)


def gradient_kernel(xt_ref, dy_ref, dg_ref, du_ref, hid_ref, theirs_ref, mine_ref):
    j = pl.program_id(0)

    def part(out_ref):
        out_ref[:SUB, :] = dot(xt_ref[...], dg_ref[...], (1, 0)).astype(BF16)
        out_ref[SUB : 2 * SUB, :] = dot(xt_ref[...], du_ref[...], (1, 0)).astype(BF16)
        down = dot(hid_ref[...].T, dy_ref[...], (1, 0)).astype(BF16)
        for f in range(SUB // PART):
            low = 2 * SUB + f * PART
            out_ref[low : low + PART, :] = down[:, f * PART : (f + 1) * PART]

    @pl.when(j == 0)
    def _():
        part(theirs_ref)

    @pl.when(j == 1)
    def _():
        part(mine_ref)


def gradients(x_t, dy, d_gate, d_up, hidden, q):
    columns = pl.BlockSpec((ROWS, PART), lambda j: (0, q + 2 * (1 - j)))
    out = pl.BlockSpec((3 * SUB, PART), lambda j: (0, 0))
    return pl.pallas_call(
        gradient_kernel,
        grid=(2,),
        in_specs=[
            pl.BlockSpec((SUB, ROWS), lambda j: (0, 0)),
            pl.BlockSpec((ROWS, SUB), lambda j: (0, 0)),
            columns,
            columns,
            columns,
        ],
        out_specs=[out, out],
        out_shape=[jax.ShapeDtypeStruct((3 * SUB, PART), BF16)] * 2,
        compiler_params=params(),
        cost_estimate=pl.CostEstimate(
            flops=3 * ROWS * SUB * SUB, bytes_accessed=10 * 2**20, transcendentals=0
        ),
    )(x_t, dy, d_gate, d_up, hidden)


def pack_kernel(odd_ref, g_ref, u_ref, d_ref, first_ref, second_ref):
    odd = odd_ref[0]
    for out_ref, p in ((first_ref, odd), (second_ref, 1 - odd)):
        out_ref[:SUB, :] = g_ref[p]
        out_ref[SUB : 2 * SUB, :] = u_ref[p]
        down = d_ref[p]
        for f in range(SUB // PART):
            low = 2 * SUB + f * PART
            out_ref[low : low + PART, :] = down[:, f * PART : (f + 1) * PART]


def unpack_kernel(odd_ref, first_ref, second_ref, g_ref, u_ref, d_ref):
    odd = odd_ref[0]
    for ref, p in ((first_ref, odd), (second_ref, 1 - odd)):
        g_ref[p] = ref[:SUB, :]
        u_ref[p] = ref[SUB : 2 * SUB, :]
        for f in range(SUB // PART):
            low = 2 * SUB + f * PART
            d_ref[p, :, f * PART : (f + 1) * PART] = ref[low : low + PART, :]


def repack(kernel, odd, arrays, shapes):
    return pl.pallas_call(
        kernel,
        in_specs=[pl.BlockSpec(memory_space=pltpu.SMEM)]
        + [pl.BlockSpec(memory_space=pltpu.VMEM)] * len(arrays),
        out_specs=[pl.BlockSpec(memory_space=pltpu.VMEM)] * len(shapes),
        out_shape=[jax.ShapeDtypeStruct(shape, BF16) for shape in shapes],
        compiler_params=pltpu.CompilerParams(vmem_limit_bytes=32 * 1024 * 1024),
        cost_estimate=pl.CostEstimate(flops=0, bytes_accessed=6 * 2**20, transcendentals=0),
    )(odd, *arrays)


def glance_kernel(a_ref, b_ref, c_ref, out_ref):
    out_ref[...] = a_ref[...] + b_ref[...] + c_ref[...]


def glance(arrays):
    corner = pl.BlockSpec((16, 128), lambda i: (0, 0))
    return pl.pallas_call(
        glance_kernel,
        grid=(1,),
        in_specs=[corner] * 3,
        out_specs=corner,
        out_shape=jax.ShapeDtypeStruct((16, 128), BF16),
        cost_estimate=pl.CostEstimate(flops=200000000000, bytes_accessed=8192, transcendentals=0),
    )(*arrays)


def params(mib=48):
    return pltpu.CompilerParams(
        dimension_semantics=("arbitrary",), vmem_limit_bytes=mib * 1024 * 1024
    )


def forward(x, own, other, seen):
    columns = pl.BlockSpec((ROWS, PART), lambda j: (0, j))
    float_out = jax.ShapeDtypeStruct((ROWS, SUB), F32)
    square = jax.ShapeDtypeStruct((SUB, SUB), BF16)
    return pl.pallas_call(
        forward_kernel,
        grid=(4,),
        in_specs=[
            pl.BlockSpec((ROWS, SUB), lambda j: (0, 0)),
        ]
        + [pl.BlockSpec((2, 3 * SUB, PART), lambda j: (0, 0, 0))] * 2
        + [pl.BlockSpec((16, 128), lambda j: (0, 0))],
        out_specs=[columns] * 3
        + [pl.BlockSpec((PART, SUB), lambda j: (j, 0))] * 2
        + [pl.BlockSpec((SUB, PART), lambda j: (0, j)), pl.BlockSpec((SUB, ROWS), lambda j: (0, 0))],
        out_shape=[float_out, float_out, jax.ShapeDtypeStruct((ROWS, SUB), BF16)]
        + [square] * 3
        + [jax.ShapeDtypeStruct((SUB, ROWS), BF16)],
        scratch_shapes=[pltpu.VMEM((3 * SUB, PART), BF16)],
        compiler_params=params(),
        cost_estimate=pl.CostEstimate(
            flops=4 * ROWS * SUB * SUB, bytes_accessed=24 * 2**20, transcendentals=ROWS * SUB
        ),
    )(x, own, other, seen)


def backward(dy, act, fac, gate_t, up_t, down_t):
    some = pl.BlockSpec((STEP, SUB), lambda i: (i, 0))
    square = pl.BlockSpec((SUB, SUB), lambda i: (0, 0))
    return pl.pallas_call(
        backward_kernel,
        grid=(ROWS // STEP,),
        in_specs=[some] * 3 + [square] * 3,
        out_specs=[some] * 3,
        out_shape=[jax.ShapeDtypeStruct((ROWS, SUB), BF16)] * 3,
        compiler_params=params(60),
        cost_estimate=pl.CostEstimate(
            flops=6 * ROWS * SUB * SUB, bytes_accessed=20 * 2**20, transcendentals=0
        ),
    )(dy, act, fac, gate_t, up_t, down_t)


def on_device(tokens, cotangent, gates, expert_ids, slots, w_gate, w_up, w_down):
    toks = tokens.shape[0]
    rows = toks * HEADS
    h = lax.axis_index("rep")

    odd = (h % 2).reshape(1)
    pieces = repack(pack_kernel, odd, (w_gate, w_up, w_down), [(3 * SUB, PART)] * 2)
    own = [lax.ppermute(pieces[q], PAIR, to_host(q)) for q in range(2)]

    def heads_first(a):
        return jnp.transpose(a, (1, 0, 2)).reshape(rows, 2)

    ids = heads_first(expert_ids)
    slot = heads_first(slots)
    gate = heads_first(gates)
    first = (((ids >> 2) & 15) * PLANES + (ids >> 6) * 4 + (ids & 3)) * CAP
    target = jnp.where(slot < CAP, first + slot, ROWS)
    place = lax.broadcasted_iota(jnp.int32, (ROWS, rows), 0)
    hit0 = target[:, 0][None, :] == place
    hit1 = target[:, 1][None, :] == place
    zero = jnp.zeros((), BF16)
    pick = (hit0 | hit1).astype(BF16)
    pick_gate = jnp.where(hit0, gate[:, 0][None, :], jnp.where(hit1, gate[:, 1][None, :], zero))

    def cut(a):
        return jnp.concatenate([a[:, i * SUB : (i + 1) * SUB] for i in range(HEADS)], 0)

    def in_plane(a):
        a = a.reshape(YX, PLANES * CAP, SUB)
        return lax.all_to_all(a, ("y", "x"), 0, 0, tiled=True).reshape(ROWS, SUB)

    def along_z(a):
        a = a.reshape(PLANES, YX * CAP, SUB)
        return lax.all_to_all(a, ("zh", "rep"), 0, 0, tiled=True).reshape(ROWS, SUB)

    row = jnp.arange(ROWS, dtype=jnp.int32)
    plane, rest = row // (YX * CAP), row % (YX * CAP)
    source = (rest // CAP) * (PLANES * CAP) + plane * CAP + rest % CAP
    regroup = (source[:, None] == row[None, :]).astype(BF16)

    x_slot = dot(pick, cut(tokens), (1, 0)).astype(BF16)
    dy_slot = dot(pick_gate, cut(cotangent), (1, 0)).astype(BF16)
    x_rows = dot(regroup, in_plane(x_slot), (1, 0)).astype(BF16)
    dy_rows = in_plane(dy_slot)
    seen = glance(own + [x_rows])
    x_rows, dy_rows, own, seen = lax.optimization_barrier((x_rows, dy_rows, own, seen))
    own = jnp.stack(own, 0)
    other = lax.ppermute(own, "core", SWAP)
    x = along_z(x_rows)
    act, fac, hidden, gate_t, up_t, down_t, x_t = forward(x, own, other, seen)
    dy = along_z(dot(regroup, dy_rows, (1, 0)).astype(BF16))
    d_gate, d_up, dx = backward(dy, act, fac, gate_t, up_t, down_t)
    dx = along_z(dx)

    sums = []
    for q in range(2):
        theirs, mine = gradients(x_t, dy, d_gate, d_up, hidden, q)
        theirs = lax.ppermute(theirs, "core", SWAP)
        sums.append((mine.astype(F32) + theirs.astype(F32)).astype(BF16))
    first = lax.ppermute(sums[0], PAIR, from_host(0))
    first, second = lax.optimization_barrier((first, sums[1]))
    back = [first, lax.ppermute(second, PAIR, from_host(1))]
    returned = in_plane(dot(regroup, dx, (0, 0)).astype(BF16))
    summed = dot(pick, returned, (0, 0)).astype(BF16)
    token_grads = jnp.concatenate([summed[i * toks : (i + 1) * toks] for i in range(HEADS)], 1)

    token_grads, back = lax.optimization_barrier((token_grads, back))
    grad_gate, grad_up, grad_down = repack(
        unpack_kernel, odd, back, [(2, SUB, PART), (2, SUB, PART), (2, PART, SUB)]
    )
    return (token_grads, grad_gate, grad_up, grad_down)


def solution(mesh):
    fine = Mesh(mesh.devices.reshape(4, 2, 4, 4, 2), AXES)
    by_token = ("rep",) + EXP
    return jax.shard_map(
        on_device,
        mesh=fine,
        in_specs=(
            P(by_token, None),
            P(by_token, None),
            P(by_token, None, None),
            P(by_token, None, None),
            P(by_token, None, None),
            P(EXP, None, "rep"),
            P(EXP, None, "rep"),
            P(EXP, "rep", None),
        ),
        out_specs=(
            P(by_token, None),
            P(EXP, None, "rep"),
            P(EXP, None, "rep"),
            P(EXP, "rep", None),
        ),
        check_vma=False,
    )
```

```python
import jax
import jax.numpy as jnp
from jax import lax
from jax.experimental import pallas as pl
from jax.experimental.pallas import tpu as pltpu
from jax.sharding import Mesh
from jax.sharding import PartitionSpec as P

HEADS = 4
CAP = 7
EXPERTS = 128
SUB = 1024
PART = 256
STEP = 448
ROWS = EXPERTS * CAP
AXES = ("rep", "zh", "y", "x", "core")
EXP = ("zh", "y", "x", "core")
PAIR = ("rep", "core")
PLANES = 8
YX = 16
SWAP = [(0, 1), (1, 0)]
F32, BF16 = jnp.float32, jnp.bfloat16


def to_host(q):
    return [
        (h * 2 + k, (2 * k + (h + q) % 2) * 2 + h // 2) for h in range(4) for k in range(2)
    ]


def from_host(q):
    return [(b, a) for a, b in to_host(q)]


def dot(a, b, over):
    return lax.dot_general(a, b, ((over[:1], over[1:]), ((), ())), preferred_element_type=F32)


def forward_kernel(
    x_ref, own_ref, other_ref, _, act_ref, fac_ref, hid_ref, gt_ref, ut_ref, dt_ref, xt_ref, w_ref
):
    j = pl.program_id(0)
    for i in range(4):

        @pl.when(j == i)
        def _():
            w_ref[...] = (own_ref, other_ref)[i // 2][i % 2]

    @pl.when(j == 0)
    def _():
        xt_ref[...] = x_ref[...].T

    def step(i, _):
        at = pl.ds(pl.multiple_of(i * STEP, STEP), STEP)
        x = x_ref[at, :]
        g = dot(x, w_ref[:SUB, :], (1, 0))
        u = dot(x, w_ref[SUB : 2 * SUB, :], (1, 0))
        sig = jax.nn.sigmoid(g)
        act = g * sig
        act_ref[at, :] = act
        fac_ref[at, :] = u * sig * (1.0 + g * (1.0 - sig))
        hid_ref[at, :] = (act * u).astype(BF16)
        return 0

    lax.fori_loop(0, ROWS // STEP, step, 0)
    gt_ref[...] = w_ref[:SUB, :].T
    ut_ref[...] = w_ref[SUB : 2 * SUB, :].T
    for f in range(SUB // PART):
        low = 2 * SUB + f * PART
        dt_ref[f * PART : (f + 1) * PART, :] = w_ref[low : low + PART, :].T


def backward_kernel(dy_ref, act_ref, fac_ref, gt_ref, ut_ref, dt_ref, dg_ref, du_ref, dx_ref):
    dh = dot(dy_ref[...], dt_ref[...], (1, 0))
    du_ref[...] = (dh * act_ref[...]).astype(BF16)
    dg_ref[...] = (dh * fac_ref[...]).astype(BF16)
    dx = dot(dg_ref[...], gt_ref[...], (1, 0)) + dot(du_ref[...], ut_ref[...], (1, 0))
    dx_ref[...] = dx.astype(BF16)


def gradient_kernel(xt_ref, dy_ref, dg_ref, du_ref, hid_ref, theirs_ref, mine_ref):
    j = pl.program_id(0)

    def part(out_ref):
        out_ref[:SUB, :] = dot(xt_ref[...], dg_ref[...], (1, 0)).astype(BF16)
        out_ref[SUB : 2 * SUB, :] = dot(xt_ref[...], du_ref[...], (1, 0)).astype(BF16)
        down = dot(hid_ref[...].T, dy_ref[...], (1, 0)).astype(BF16)
        for f in range(SUB // PART):
            low = 2 * SUB + f * PART
            out_ref[low : low + PART, :] = down[:, f * PART : (f + 1) * PART]

    @pl.when(j == 0)
    def _():
        part(theirs_ref)

    @pl.when(j == 1)
    def _():
        part(mine_ref)


def gradients(x_t, dy, d_gate, d_up, hidden, q):
    columns = pl.BlockSpec((ROWS, PART), lambda j: (0, q + 2 * (1 - j)))
    out = pl.BlockSpec((3 * SUB, PART), lambda j: (0, 0))
    return pl.pallas_call(
        gradient_kernel,
        grid=(2,),
        in_specs=[
            pl.BlockSpec((SUB, ROWS), lambda j: (0, 0)),
            pl.BlockSpec((ROWS, SUB), lambda j: (0, 0)),
            columns,
            columns,
            columns,
        ],
        out_specs=[out, out],
        out_shape=[jax.ShapeDtypeStruct((3 * SUB, PART), BF16)] * 2,
        compiler_params=params(),
        cost_estimate=pl.CostEstimate(
            flops=3 * ROWS * SUB * SUB, bytes_accessed=10 * 2**20, transcendentals=0
        ),
    )(x_t, dy, d_gate, d_up, hidden)


def pack_kernel(odd_ref, g_ref, u_ref, d_ref, first_ref, second_ref):
    odd = odd_ref[0]
    for out_ref, p in ((first_ref, odd), (second_ref, 1 - odd)):
        out_ref[:SUB, :] = g_ref[p]
        out_ref[SUB : 2 * SUB, :] = u_ref[p]
        down = d_ref[p]
        for f in range(SUB // PART):
            low = 2 * SUB + f * PART
            out_ref[low : low + PART, :] = down[:, f * PART : (f + 1) * PART]


def unpack_kernel(odd_ref, first_ref, second_ref, g_ref, u_ref, d_ref):
    odd = odd_ref[0]
    for ref, p in ((first_ref, odd), (second_ref, 1 - odd)):
        g_ref[p] = ref[:SUB, :]
        u_ref[p] = ref[SUB : 2 * SUB, :]
        for f in range(SUB // PART):
            low = 2 * SUB + f * PART
            d_ref[p, :, f * PART : (f + 1) * PART] = ref[low : low + PART, :]


def repack(kernel, odd, arrays, shapes):
    return pl.pallas_call(
        kernel,
        in_specs=[pl.BlockSpec(memory_space=pltpu.SMEM)]
        + [pl.BlockSpec(memory_space=pltpu.VMEM)] * len(arrays),
        out_specs=[pl.BlockSpec(memory_space=pltpu.VMEM)] * len(shapes),
        out_shape=[jax.ShapeDtypeStruct(shape, BF16) for shape in shapes],
        compiler_params=pltpu.CompilerParams(vmem_limit_bytes=32 * 1024 * 1024),
        cost_estimate=pl.CostEstimate(flops=0, bytes_accessed=6 * 2**20, transcendentals=0),
    )(odd, *arrays)


def glance_kernel(a_ref, b_ref, c_ref, out_ref):
    out_ref[...] = a_ref[...] + b_ref[...] + c_ref[...]


def glance(arrays):
    corner = pl.BlockSpec((16, 128), lambda i: (0, 0))
    return pl.pallas_call(
        glance_kernel,
        grid=(1,),
        in_specs=[corner] * 3,
        out_specs=corner,
        out_shape=jax.ShapeDtypeStruct((16, 128), BF16),
        cost_estimate=pl.CostEstimate(flops=200000000000, bytes_accessed=8192, transcendentals=0),
    )(*arrays)


def params(mib=48):
    return pltpu.CompilerParams(
        dimension_semantics=("arbitrary",), vmem_limit_bytes=mib * 1024 * 1024
    )


def forward(x, own, other, seen):
    columns = pl.BlockSpec((ROWS, PART), lambda j: (0, j))
    float_out = jax.ShapeDtypeStruct((ROWS, SUB), F32)
    square = jax.ShapeDtypeStruct((SUB, SUB), BF16)
    return pl.pallas_call(
        forward_kernel,
        grid=(4,),
        in_specs=[
            pl.BlockSpec((ROWS, SUB), lambda j: (0, 0)),
        ]
        + [pl.BlockSpec((2, 3 * SUB, PART), lambda j: (0, 0, 0))] * 2
        + [pl.BlockSpec((16, 128), lambda j: (0, 0))],
        out_specs=[columns] * 3
        + [pl.BlockSpec((PART, SUB), lambda j: (j, 0))] * 2
        + [pl.BlockSpec((SUB, PART), lambda j: (0, j)), pl.BlockSpec((SUB, ROWS), lambda j: (0, 0))],
        out_shape=[float_out, float_out, jax.ShapeDtypeStruct((ROWS, SUB), BF16)]
        + [square] * 3
        + [jax.ShapeDtypeStruct((SUB, ROWS), BF16)],
        scratch_shapes=[pltpu.VMEM((3 * SUB, PART), BF16)],
        compiler_params=params(),
        cost_estimate=pl.CostEstimate(
            flops=4 * ROWS * SUB * SUB, bytes_accessed=24 * 2**20, transcendentals=ROWS * SUB
        ),
    )(x, own, other, seen)


def backward(dy, act, fac, gate_t, up_t, down_t):
    some = pl.BlockSpec((STEP, SUB), lambda i: (i, 0))
    square = pl.BlockSpec((SUB, SUB), lambda i: (0, 0))
    return pl.pallas_call(
        backward_kernel,
        grid=(ROWS // STEP,),
        in_specs=[some] * 3 + [square] * 3,
        out_specs=[some] * 3,
        out_shape=[jax.ShapeDtypeStruct((ROWS, SUB), BF16)] * 3,
        compiler_params=params(60),
        cost_estimate=pl.CostEstimate(
            flops=6 * ROWS * SUB * SUB, bytes_accessed=20 * 2**20, transcendentals=0
        ),
    )(dy, act, fac, gate_t, up_t, down_t)


def on_device(tokens, cotangent, gates, expert_ids, slots, w_gate, w_up, w_down):
    toks = tokens.shape[0]
    rows = toks * HEADS
    h = lax.axis_index("rep")

    odd = (h % 2).reshape(1)
    pieces = repack(pack_kernel, odd, (w_gate, w_up, w_down), [(3 * SUB, PART)] * 2)
    own = [lax.ppermute(pieces[q], PAIR, to_host(q)) for q in range(2)]

    def heads_first(a):
        return jnp.transpose(a, (1, 0, 2)).reshape(rows, 2)

    ids = heads_first(expert_ids)
    slot = heads_first(slots)
    gate = heads_first(gates)
    first = (((ids >> 2) & 15) * PLANES + (ids >> 6) * 4 + (ids & 3)) * CAP
    target = jnp.where(slot < CAP, first + slot, ROWS)
    place = lax.broadcasted_iota(jnp.int32, (ROWS, rows), 0)
    hit0 = target[:, 0][None, :] == place
    hit1 = target[:, 1][None, :] == place
    zero = jnp.zeros((), BF16)
    pick = (hit0 | hit1).astype(BF16)
    pick_gate = jnp.where(hit0, gate[:, 0][None, :], jnp.where(hit1, gate[:, 1][None, :], zero))

    def cut(a):
        return jnp.concatenate([a[:, i * SUB : (i + 1) * SUB] for i in range(HEADS)], 0)

    def in_plane(a):
        a = a.reshape(YX, PLANES * CAP, SUB)
        return lax.all_to_all(a, ("y", "x"), 0, 0, tiled=True).reshape(ROWS, SUB)

    def along_z(a):
        a = a.reshape(PLANES, YX * CAP, SUB)
        return lax.all_to_all(a, ("zh", "rep"), 0, 0, tiled=True).reshape(ROWS, SUB)

    row = jnp.arange(ROWS, dtype=jnp.int32)
    plane, rest = row // (YX * CAP), row % (YX * CAP)
    source = (rest // CAP) * (PLANES * CAP) + plane * CAP + rest % CAP
    regroup = (source[:, None] == row[None, :]).astype(BF16)

    x_slot = dot(pick, cut(tokens), (1, 0)).astype(BF16)
    dy_slot = dot(pick_gate, cut(cotangent), (1, 0)).astype(BF16)
    x_rows = dot(regroup, in_plane(x_slot), (1, 0)).astype(BF16)
    dy_rows = in_plane(dy_slot)
    seen = glance([own[0], x_rows, x_rows])
    x_rows, dy_rows, own[0], seen = lax.optimization_barrier((x_rows, dy_rows, own[0], seen))
    seen = glance([own[1], seen, seen])
    own[1], seen = lax.optimization_barrier((own[1], seen))
    own = jnp.stack(own, 0)
    other = lax.ppermute(own, "core", SWAP)
    x = along_z(x_rows)
    act, fac, hidden, gate_t, up_t, down_t, x_t = forward(x, own, other, seen)
    dy = along_z(dot(regroup, dy_rows, (1, 0)).astype(BF16))
    d_gate, d_up, dx = backward(dy, act, fac, gate_t, up_t, down_t)
    dx = along_z(dx)

    sums = []
    for q in range(2):
        theirs, mine = gradients(x_t, dy, d_gate, d_up, hidden, q)
        theirs = lax.ppermute(theirs, "core", SWAP)
        sums.append((mine.astype(F32) + theirs.astype(F32)).astype(BF16))
    first = lax.ppermute(sums[0], PAIR, from_host(0))
    first, second = lax.optimization_barrier((first, sums[1]))
    back = [first, lax.ppermute(second, PAIR, from_host(1))]
    returned = in_plane(dot(regroup, dx, (0, 0)).astype(BF16))
    summed = dot(pick, returned, (0, 0)).astype(BF16)
    token_grads = jnp.concatenate([summed[i * toks : (i + 1) * toks] for i in range(HEADS)], 1)

    token_grads, back = lax.optimization_barrier((token_grads, back))
    grad_gate, grad_up, grad_down = repack(
        unpack_kernel, odd, back, [(2, SUB, PART), (2, SUB, PART), (2, PART, SUB)]
    )
    return (token_grads, grad_gate, grad_up, grad_down)


def solution(mesh):
    fine = Mesh(mesh.devices.reshape(4, 2, 4, 4, 2), AXES)
    by_token = ("rep",) + EXP
    return jax.shard_map(
        on_device,
        mesh=fine,
        in_specs=(
            P(by_token, None),
            P(by_token, None),
            P(by_token, None, None),
            P(by_token, None, None),
            P(by_token, None, None),
            P(EXP, None, "rep"),
            P(EXP, None, "rep"),
            P(EXP, "rep", None),
        ),
        out_specs=(
            P(by_token, None),
            P(EXP, None, "rep"),
            P(EXP, None, "rep"),
            P(EXP, "rep", None),
        ),
        check_vma=False,
    )
```

```python
import jax
import jax.numpy as jnp
from jax import lax
from jax.experimental import pallas as pl
from jax.experimental.pallas import tpu as pltpu
from jax.sharding import Mesh
from jax.sharding import PartitionSpec as P

HEADS = 4
CAP = 7
EXPERTS = 128
SUB = 1024
PART = 256
STEP = 448
ROWS = EXPERTS * CAP
AXES = ("rep", "zh", "y", "x", "core")
EXP = ("zh", "y", "x", "core")
PAIR = ("rep", "core")
PLANES = 8
YX = 16
SWAP = [(0, 1), (1, 0)]
F32, BF16 = jnp.float32, jnp.bfloat16


def to_host(q):
    return [
        (h * 2 + k, (2 * k + (h + q) % 2) * 2 + h // 2) for h in range(4) for k in range(2)
    ]


def from_host(q):
    return [(b, a) for a, b in to_host(q)]


def dot(a, b, over):
    return lax.dot_general(a, b, ((over[:1], over[1:]), ((), ())), preferred_element_type=F32)


def forward_kernel(
    x_ref, own_ref, other_ref, _, act_ref, fac_ref, hid_ref, gu_ref, dt_ref, xt_ref, w_ref
):
    j = pl.program_id(0)
    for i in range(4):

        @pl.when(j == i)
        def _():
            w_ref[...] = (own_ref, other_ref)[i // 2][i % 2]

    @pl.when(j == 0)
    def _():
        xt_ref[...] = x_ref[...].T

    def step(i, _):
        at = pl.ds(pl.multiple_of(i * STEP, STEP), STEP)
        x = x_ref[at, :]
        g = dot(x, w_ref[:SUB, :], (1, 0))
        u = dot(x, w_ref[SUB : 2 * SUB, :], (1, 0))
        sig = jax.nn.sigmoid(g)
        act = g * sig
        act_ref[at, :] = act
        fac_ref[at, :] = u * sig * (1.0 + g * (1.0 - sig))
        hid_ref[at, :] = (act * u).astype(BF16)
        return 0

    lax.fori_loop(0, ROWS // STEP, step, 0)
    gu_ref[0] = w_ref[:SUB, :].T
    gu_ref[1] = w_ref[SUB : 2 * SUB, :].T
    for f in range(SUB // PART):
        low = 2 * SUB + f * PART
        dt_ref[f * PART : (f + 1) * PART, :] = w_ref[low : low + PART, :].T


def backward_kernel(dy_ref, act_ref, fac_ref, gu_ref, dt_ref, dg_ref, du_ref, dx_ref, both_ref):
    dh = dot(dy_ref[...], dt_ref[...], (1, 0))
    d_gate = (dh * fac_ref[...]).astype(BF16)
    d_up = (dh * act_ref[...]).astype(BF16)
    dg_ref[...] = d_gate
    du_ref[...] = d_up
    both_ref[:, :SUB] = d_gate
    both_ref[:, SUB:] = d_up
    dx_ref[...] = dot(both_ref[...], gu_ref[...].reshape(2 * SUB, SUB), (1, 0)).astype(BF16)


def gradient_kernel(xt_ref, dy_ref, dg_ref, du_ref, hid_ref, theirs_ref, mine_ref):
    j = pl.program_id(0)

    def part(out_ref):
        out_ref[:SUB, :] = dot(xt_ref[...], dg_ref[...], (1, 0)).astype(BF16)
        out_ref[SUB : 2 * SUB, :] = dot(xt_ref[...], du_ref[...], (1, 0)).astype(BF16)
        down = dot(hid_ref[...].T, dy_ref[...], (1, 0)).astype(BF16)
        for f in range(SUB // PART):
            low = 2 * SUB + f * PART
            out_ref[low : low + PART, :] = down[:, f * PART : (f + 1) * PART]

    @pl.when(j == 0)
    def _():
        part(theirs_ref)

    @pl.when(j == 1)
    def _():
        part(mine_ref)


def gradients(x_t, dy, d_gate, d_up, hidden, q):
    columns = pl.BlockSpec((ROWS, PART), lambda j: (0, q + 2 * (1 - j)))
    out = pl.BlockSpec((3 * SUB, PART), lambda j: (0, 0))
    return pl.pallas_call(
        gradient_kernel,
        grid=(2,),
        in_specs=[
            pl.BlockSpec((SUB, ROWS), lambda j: (0, 0)),
            pl.BlockSpec((ROWS, SUB), lambda j: (0, 0)),
            columns,
            columns,
            columns,
        ],
        out_specs=[out, out],
        out_shape=[jax.ShapeDtypeStruct((3 * SUB, PART), BF16)] * 2,
        compiler_params=params(),
        cost_estimate=pl.CostEstimate(
            flops=3 * ROWS * SUB * SUB, bytes_accessed=10 * 2**20, transcendentals=0
        ),
    )(x_t, dy, d_gate, d_up, hidden)


def pack_kernel(odd_ref, g_ref, u_ref, d_ref, first_ref, second_ref):
    odd = odd_ref[0]
    for out_ref, p in ((first_ref, odd), (second_ref, 1 - odd)):
        out_ref[:SUB, :] = g_ref[p]
        out_ref[SUB : 2 * SUB, :] = u_ref[p]
        down = d_ref[p]
        for f in range(SUB // PART):
            low = 2 * SUB + f * PART
            out_ref[low : low + PART, :] = down[:, f * PART : (f + 1) * PART]


def unpack_kernel(odd_ref, first_ref, second_ref, g_ref, u_ref, d_ref):
    odd = odd_ref[0]
    for ref, p in ((first_ref, odd), (second_ref, 1 - odd)):
        g_ref[p] = ref[:SUB, :]
        u_ref[p] = ref[SUB : 2 * SUB, :]
        for f in range(SUB // PART):
            low = 2 * SUB + f * PART
            d_ref[p, :, f * PART : (f + 1) * PART] = ref[low : low + PART, :]


def repack(kernel, odd, arrays, shapes):
    return pl.pallas_call(
        kernel,
        in_specs=[pl.BlockSpec(memory_space=pltpu.SMEM)]
        + [pl.BlockSpec(memory_space=pltpu.VMEM)] * len(arrays),
        out_specs=[pl.BlockSpec(memory_space=pltpu.VMEM)] * len(shapes),
        out_shape=[jax.ShapeDtypeStruct(shape, BF16) for shape in shapes],
        compiler_params=pltpu.CompilerParams(vmem_limit_bytes=32 * 1024 * 1024),
        cost_estimate=pl.CostEstimate(flops=0, bytes_accessed=6 * 2**20, transcendentals=0),
    )(odd, *arrays)


def glance_kernel(a_ref, b_ref, c_ref, out_ref):
    out_ref[...] = a_ref[...] + b_ref[...] + c_ref[...]


def glance(arrays):
    corner = pl.BlockSpec((16, 128), lambda i: (0, 0))
    return pl.pallas_call(
        glance_kernel,
        grid=(1,),
        in_specs=[corner] * 3,
        out_specs=corner,
        out_shape=jax.ShapeDtypeStruct((16, 128), BF16),
        cost_estimate=pl.CostEstimate(flops=200000000000, bytes_accessed=8192, transcendentals=0),
    )(*arrays)


def params(mib=48):
    return pltpu.CompilerParams(
        dimension_semantics=("arbitrary",), vmem_limit_bytes=mib * 1024 * 1024
    )


def forward(x, own, other, seen):
    columns = pl.BlockSpec((ROWS, PART), lambda j: (0, j))
    float_out = jax.ShapeDtypeStruct((ROWS, SUB), F32)
    square = jax.ShapeDtypeStruct((SUB, SUB), BF16)
    return pl.pallas_call(
        forward_kernel,
        grid=(4,),
        in_specs=[
            pl.BlockSpec((ROWS, SUB), lambda j: (0, 0)),
        ]
        + [pl.BlockSpec((2, 3 * SUB, PART), lambda j: (0, 0, 0))] * 2
        + [pl.BlockSpec((16, 128), lambda j: (0, 0))],
        out_specs=[columns] * 3
        + [pl.BlockSpec((2, PART, SUB), lambda j: (0, j, 0))]
        + [pl.BlockSpec((SUB, PART), lambda j: (0, j)), pl.BlockSpec((SUB, ROWS), lambda j: (0, 0))],
        out_shape=[float_out, float_out, jax.ShapeDtypeStruct((ROWS, SUB), BF16)]
        + [jax.ShapeDtypeStruct((2, SUB, SUB), BF16), square]
        + [jax.ShapeDtypeStruct((SUB, ROWS), BF16)],
        scratch_shapes=[pltpu.VMEM((3 * SUB, PART), BF16)],
        compiler_params=params(),
        cost_estimate=pl.CostEstimate(
            flops=4 * ROWS * SUB * SUB, bytes_accessed=24 * 2**20, transcendentals=ROWS * SUB
        ),
    )(x, own, other, seen)


def backward(dy, act, fac, both_t, down_t):
    some = pl.BlockSpec((STEP, SUB), lambda i: (i, 0))
    square = pl.BlockSpec((SUB, SUB), lambda i: (0, 0))
    return pl.pallas_call(
        backward_kernel,
        grid=(ROWS // STEP,),
        in_specs=[some] * 3 + [pl.BlockSpec((2, SUB, SUB), lambda i: (0, 0, 0)), square],
        out_specs=[some] * 3,
        out_shape=[jax.ShapeDtypeStruct((ROWS, SUB), BF16)] * 3,
        scratch_shapes=[pltpu.VMEM((STEP, 2 * SUB), BF16)],
        compiler_params=params(60),
        cost_estimate=pl.CostEstimate(
            flops=6 * ROWS * SUB * SUB, bytes_accessed=20 * 2**20, transcendentals=0
        ),
    )(dy, act, fac, both_t, down_t)


def on_device(tokens, cotangent, gates, expert_ids, slots, w_gate, w_up, w_down):
    toks = tokens.shape[0]
    rows = toks * HEADS
    h = lax.axis_index("rep")

    odd = (h % 2).reshape(1)
    pieces = repack(pack_kernel, odd, (w_gate, w_up, w_down), [(3 * SUB, PART)] * 2)
    own = [lax.ppermute(pieces[q], PAIR, to_host(q)) for q in range(2)]

    def heads_first(a):
        return jnp.transpose(a, (1, 0, 2)).reshape(rows, 2)

    ids = heads_first(expert_ids)
    slot = heads_first(slots)
    gate = heads_first(gates)
    first = (((ids >> 2) & 15) * PLANES + (ids >> 6) * 4 + (ids & 3)) * CAP
    target = jnp.where(slot < CAP, first + slot, ROWS)
    place = lax.broadcasted_iota(jnp.int32, (ROWS, rows), 0)
    hit0 = target[:, 0][None, :] == place
    hit1 = target[:, 1][None, :] == place
    zero = jnp.zeros((), BF16)
    pick = (hit0 | hit1).astype(BF16)
    pick_gate = jnp.where(hit0, gate[:, 0][None, :], jnp.where(hit1, gate[:, 1][None, :], zero))

    def cut(a):
        return jnp.concatenate([a[:, i * SUB : (i + 1) * SUB] for i in range(HEADS)], 0)

    def in_plane(a):
        a = a.reshape(YX, PLANES * CAP, SUB)
        return lax.all_to_all(a, ("y", "x"), 0, 0, tiled=True).reshape(ROWS, SUB)

    def along_z(a):
        a = a.reshape(PLANES, YX * CAP, SUB)
        return lax.all_to_all(a, ("zh", "rep"), 0, 0, tiled=True).reshape(ROWS, SUB)

    row = jnp.arange(ROWS, dtype=jnp.int32)
    plane, rest = row // (YX * CAP), row % (YX * CAP)
    source = (rest // CAP) * (PLANES * CAP) + plane * CAP + rest % CAP
    regroup = (source[:, None] == row[None, :]).astype(BF16)

    x_slot = dot(pick, cut(tokens), (1, 0)).astype(BF16)
    dy_slot = dot(pick_gate, cut(cotangent), (1, 0)).astype(BF16)
    x_rows = dot(regroup, in_plane(x_slot), (1, 0)).astype(BF16)
    dy_rows = in_plane(dy_slot)
    seen = glance([own[0], x_rows, x_rows])
    x_rows, dy_rows, own[0], seen = lax.optimization_barrier((x_rows, dy_rows, own[0], seen))
    seen = glance([own[1], seen, seen])
    own[1], seen = lax.optimization_barrier((own[1], seen))
    own = jnp.stack(own, 0)
    other = lax.ppermute(own, "core", SWAP)
    x = along_z(x_rows)
    act, fac, hidden, both_t, down_t, x_t = forward(x, own, other, seen)
    dy = along_z(dot(regroup, dy_rows, (1, 0)).astype(BF16))
    d_gate, d_up, dx = backward(dy, act, fac, both_t, down_t)
    dx = along_z(dx)

    sums = []
    for q in range(2):
        theirs, mine = gradients(x_t, dy, d_gate, d_up, hidden, q)
        theirs = lax.ppermute(theirs, "core", SWAP)
        sums.append((mine.astype(F32) + theirs.astype(F32)).astype(BF16))
    first = lax.ppermute(sums[0], PAIR, from_host(0))
    first, second = lax.optimization_barrier((first, sums[1]))
    back = [first, lax.ppermute(second, PAIR, from_host(1))]
    returned = in_plane(dot(regroup, dx, (0, 0)).astype(BF16))
    summed = dot(pick, returned, (0, 0)).astype(BF16)
    token_grads = jnp.concatenate([summed[i * toks : (i + 1) * toks] for i in range(HEADS)], 1)

    token_grads, back = lax.optimization_barrier((token_grads, back))
    grad_gate, grad_up, grad_down = repack(
        unpack_kernel, odd, back, [(2, SUB, PART), (2, SUB, PART), (2, PART, SUB)]
    )
    return (token_grads, grad_gate, grad_up, grad_down)


def solution(mesh):
    fine = Mesh(mesh.devices.reshape(4, 2, 4, 4, 2), AXES)
    by_token = ("rep",) + EXP
    return jax.shard_map(
        on_device,
        mesh=fine,
        in_specs=(
            P(by_token, None),
            P(by_token, None),
            P(by_token, None, None),
            P(by_token, None, None),
            P(by_token, None, None),
            P(EXP, None, "rep"),
            P(EXP, None, "rep"),
            P(EXP, "rep", None),
        ),
        out_specs=(
            P(by_token, None),
            P(EXP, None, "rep"),
            P(EXP, None, "rep"),
            P(EXP, "rep", None),
        ),
        check_vma=False,
    )
```
